128 devices in a mesh: face: 4 (over y_hi, core), tile: 32 (over y_lo, x, z).
Axes of the slice: x: 4, y: 4 (y_hi: 2, y_lo: 2; y = y_hi * 2 + y_lo), z: 4, core: 2. Of those that a mesh axis runs over, the one named last changes fastest.
Arguments:
- coarse_features: bfloat16 [3, 128, 1024, 256], P(None, None, ('face', 'tile')), may hold values from -6 to 6
- skip_features: bfloat16 [3, 64, 2048, 512], P(None, None, ('face', 'tile')), may hold values from -6 to 6
- up_weight: bfloat16 [2, 2, 64, 128], replicated, may hold values from -0.5 to 0.5
- up_bias: float32 [64], replicated, may hold values from -3 to 3
- first_weight: bfloat16 [3, 3, 64, 128], replicated, may hold values from -0.1875 to 0.1875
- first_bias: float32 [64], replicated, may hold values from -3 to 3
- second_weight: bfloat16 [3, 3, 64, 64], replicated, may hold values from -0.25 to 0.25
- second_bias: float32 [64], replicated, may hold values from -3 to 3
- head_weight: bfloat16 [8, 64], replicated, may hold values from -0.75 to 0.75
- head_bias: float32 [8], replicated, may hold values from -3 to 3
- land_mask: int32 [2048, 512], P(('face', 'tile')), may hold values from 0 to 1, as said below
- block_target: int32 [8192], P(('face', 'tile')), may hold values from -1 to 5631, as said below
Outputs:
- surface_flux: float32 [3, 8, 2048, 512], P(None, None, ('face', 'tile'))
- ocean_flux: float32 [5632, 3, 8, 128], P(('face', 'tile'))
The draws below stay inside these ranges and needn't reach their ends.
Inputs may be any that keep to these rules, and one draw needn't show every extreme that they name: `land_mask`: 1 marks sea; every pixel of a block whose block_target is -1 is 0. `block_target`: -1 marks a block without sea; every value 0 to 5631 occurs exactly once; value // 44 is the owner, the device of that index along face+tile; the 64 blocks of one device send at most 1 block to any one owner, and this largest count of 1 is reached; some device has no block at -1.
All inputs are finite; a program needn't handle non-finite values.
Results may differ from the reference program's by a relative error of at most 0.007.
Values may be sent and summed in bfloat16 or wider, within the bound.
No kernel may reach another device: no remote copies, remote signals or barrier semaphores. Data moves between devices by JAX's collectives and lax.ppermute only.
A program may use at most 192 MiB of HBM per device.

```python
import jax
import jax.numpy as jnp
from jax import lax

B = 3
CI = 128
CO = 64
NF = 8
BLOCK = 128
NSIDE = 512
BLK_DEV = 64
OWNERS = 128
CAP = 44
N_FACE = 4


def wet_blocks(key):
    bias_key, chosen_key, noise_key = jax.random.split(key, 3)
    device_bias = jax.random.randint(bias_key, (OWNERS,), 0, 4)
    chosen = jax.random.randint(chosen_key, (), 0, OWNERS)
    device_bias = jnp.where(jnp.arange(OWNERS) == chosen, 7, device_bias)
    total_blocks = OWNERS * BLK_DEV
    scores = jnp.repeat(device_bias, BLK_DEV) * 65536 + jax.random.randint(noise_key, (total_blocks,), 0, 65536)
    sorted_ids = jnp.argsort(-scores, stable=True)
    rank_of = jnp.zeros((total_blocks,), jnp.int32).at[sorted_ids].set(jnp.arange(total_blocks, dtype=jnp.int32))
    return rank_of < OWNERS * CAP


def draw_land_mask(key, part):
    is_wet = wet_blocks(key)
    key = jax.random.fold_in(key, 11)
    sea_draw = jax.random.randint(key, (N_FACE * NSIDE, NSIDE), 0, 100) < 85
    wet_pixels = jnp.repeat(is_wet.reshape(N_FACE * NSIDE, NSIDE // BLOCK), BLOCK, axis=1)
    return (sea_draw & wet_pixels).astype(jnp.int32)


def draw_block_target(key, part):
    is_wet = wet_blocks(key)
    rank_of = jnp.cumsum(is_wet.astype(jnp.int32)) - 1
    return jnp.where(is_wet, rank_of % OWNERS * CAP + rank_of // OWNERS, -1).astype(jnp.int32)


def level_of(rng, shape, cuts, low, top_value):
    def one(position, blocks):
        draws = jax.random.uniform(jax.random.fold_in(jax.random.fold_in(rng, 6), position), (blocks,), jnp.float32, low / len(cuts), top_value / len(cuts))
        return jnp.repeat(jnp.exp(draws), shape[position] // blocks).reshape((-1,) + (1,) * (len(shape) - position - 1))

    level = one(*cuts[0])
    for cut in cuts[1:]:
        level = level * one(*cut)
    return level


def bell_draw(stream_key, shape, spread, most, pieces=(), kind=jnp.bfloat16):
    factor_of = level_of(stream_key, shape, pieces, -0.22, 0.18) if pieces else 1.0
    drawn = jax.random.normal(stream_key, shape, jnp.float32) * spread * factor_of
    return jnp.minimum(jnp.maximum(drawn, -most), most).astype(kind)


def setup_inputs(seed: int = 0) -> dict:
    streams_of = jax.random.split(jax.random.key(seed), 13)
    return {
        "coarse_features": bell_draw(streams_of[0], (B, CI, N_FACE * NSIDE // 2, NSIDE // 2), 1.0, 6.0, ((2, 128),)),
        "skip_features": bell_draw(streams_of[1], (B, CO, N_FACE * NSIDE, NSIDE), 1.0, 6.0, ((2, 128),)),
        "up_weight": bell_draw(streams_of[2], (2, 2, CO, CI), CI ** -0.5, 0.5),
        "up_bias": bell_draw(streams_of[3], (CO,), 0.5, 3.0, (), jnp.float32),
        "first_weight": bell_draw(streams_of[4], (3, 3, CO, 2 * CO), (18 * CO) ** -0.5, 0.1875),
        "first_bias": bell_draw(streams_of[5], (CO,), 0.5, 3.0, (), jnp.float32),
        "second_weight": bell_draw(streams_of[6], (3, 3, CO, CO), (9 * CO) ** -0.5, 0.25),
        "second_bias": bell_draw(streams_of[7], (CO,), 0.5, 3.0, (), jnp.float32),
        "head_weight": bell_draw(streams_of[8], (NF, CO), CO ** -0.5, 0.75),
        "head_bias": bell_draw(streams_of[9], (NF,), 0.5, 3.0, (), jnp.float32),
        "land_mask": draw_land_mask(jax.random.fold_in(streams_of[12], 71), 0),
        "block_target": draw_block_target(jax.random.fold_in(streams_of[12], 71), 0),
    }


def face_padding(values):
    channels = values.shape[0]
    side = values.shape[2]
    face_grid = values.reshape(channels, N_FACE, side, side)
    next_edge = jnp.roll(face_grid, -1, axis=1)[:, :, side - 1, :]
    prev_edge = jnp.roll(face_grid, 1, axis=1)[:, :, :, side - 1]
    zero_column = jnp.zeros((channels, N_FACE, side, 1), values.dtype)
    widened = jnp.concatenate([zero_column, face_grid, next_edge[:, :, :, None]], axis=3)
    corner = jnp.zeros((channels, N_FACE, 1, 1), values.dtype)
    bottom = jnp.concatenate([corner, prev_edge[:, :, None, :], corner], axis=3)
    top_row = jnp.zeros((channels, N_FACE, 1, side + 2), values.dtype)
    return jnp.concatenate([top_row, widened, bottom], axis=2)


def conv_layer(inputs, weight, bias):
    side = inputs.shape[3]
    out_channels = weight.shape[2]

    def one_member(sample):
        padded = face_padding(sample.astype(jnp.float32))
        summed = jnp.zeros((out_channels, N_FACE, side, side), jnp.float32)
        for row_tap in range(3):
            for col_tap in range(3):
                summed = summed + jnp.einsum("oc,cfxy->ofxy", weight[row_tap, col_tap].astype(jnp.float32), padded[:, :, row_tap:row_tap + side, col_tap:col_tap + side])
        result = jax.nn.silu(summed + bias[:, None, None, None])
        return result.reshape(out_channels, N_FACE * side, side).astype(jnp.bfloat16)

    return lax.map(one_member, inputs)


def reference(coarse_features, skip_features, up_weight, up_bias, first_weight, first_bias, second_weight, second_bias, head_weight, head_bias, land_mask, block_target):
    members = coarse_features.shape[0]
    upsampled = jnp.einsum("aeoc,bcij->boiaje", up_weight.astype(jnp.float32), coarse_features.astype(jnp.float32))
    upsampled = upsampled.reshape(members, CO, 2 * coarse_features.shape[2], 2 * coarse_features.shape[3])
    upsampled = (upsampled + up_bias[None, :, None, None]).astype(jnp.bfloat16)
    joined = jnp.concatenate([upsampled, skip_features], axis=1)
    first = conv_layer(joined, first_weight, first_bias)
    second = conv_layer(first, second_weight, second_bias)
    surface_flux = jnp.einsum("fc,bcxy->bfxy", head_weight.astype(jnp.float32), second.astype(jnp.float32)) + head_bias[None, :, None, None]
    masked = surface_flux * land_mask.astype(jnp.float32)[None, None]
    row_total = masked.shape[2]
    blocks = masked.reshape(members, NF, row_total, NSIDE // BLOCK, BLOCK).transpose(2, 3, 0, 1, 4).reshape(-1, members, NF, BLOCK)
    target = jnp.where(block_target < 0, OWNERS * CAP, block_target).astype(jnp.int32)
    ocean_flux = jnp.zeros((OWNERS * CAP, members, NF, BLOCK), jnp.float32).at[target].set(blocks, mode="drop")
    return surface_flux, ocean_flux
```

```python
import jax
import jax.numpy as jnp
from jax import lax
from jax.experimental import pallas as pl
from jax.experimental.pallas import tpu as pltpu
from jax.sharding import PartitionSpec as P

BF = jnp.bfloat16
F32 = jnp.float32
ROWS = 16
COLS = 512
BLOCK = 128
CAP = 44
VMEM_LIMIT = 56 * 1024 * 1024


def dot(a, b):
    return jnp.dot(a, b, preferred_element_type=F32)


def silu(v):
    half = 0.5 * v
    return half * jnp.tanh(half) + half


def lanes_of(shape):
    return lax.broadcasted_iota(jnp.int32, shape, len(shape) - 1)


def wide(column, tiles):
    return jnp.concatenate([column] * tiles, axis=1)


def taps(row):
    lane = lanes_of(row.shape)
    zero = jnp.zeros_like(row)
    before = jnp.where(lane == 0, zero, pltpu.roll(row, 1, 1))
    after = jnp.where(lane == COLS - 1, zero, pltpu.roll(row, COLS - 1, 1))
    return jnp.concatenate([before, row, after], axis=0)


def spread(coarse):
    lane = lanes_of((128, 128))
    parts = [
        jnp.take_along_axis(coarse[:, 128 * p : 128 * p + 128], lane // 2 + 64 * h, axis=1)
        for p in range(2)
        for h in range(2)
    ]
    even = lane % 2 == 0
    zero = jnp.zeros((128, 128), F32)
    top = jnp.concatenate([jnp.where(even, part, zero) for part in parts], axis=1)
    low = jnp.concatenate([jnp.where(even, zero, part) for part in parts], axis=1)
    return jnp.concatenate([top, low], axis=0).astype(BF)


def up_rows(up_ref):
    return jnp.concatenate(
        [jnp.concatenate([up_ref[a, 0], up_ref[a, 1]], axis=1) for a in range(2)], axis=0
    )


def row_taps(weight_ref, r):
    return jnp.concatenate([weight_ref[r, s] for s in range(3)], axis=1)


def turned_taps(weight_ref, r):
    return jnp.concatenate([weight_ref[s, 2 - r] for s in range(3)], axis=1)


def pack_kernel(coarse_ref, skip_ref, up_ref, down_ref, send_ref, col_ref, row_ref, skip_t, coarse_t):
    last_tile = lax.axis_size("tile") - 1
    tile = lax.axis_index("tile")
    rows = jnp.swapaxes(skip_ref[0], 0, 1)
    coarse_rows = jnp.swapaxes(coarse_ref[0], 0, 1)

    def pair(row):
        return jnp.concatenate([row[:64], row[64:]], axis=1)

    up_ref[0, 0] = rows[0]
    up_ref[0, 1] = rows[1]
    up_ref[0, 2] = pair(coarse_rows[0])
    down_ref[0, 0] = rows[14]
    down_ref[0, 1] = rows[15]
    down_ref[0, 2] = pair(coarse_rows[7])

    lane = lanes_of((128, 128))
    skip_cols = jnp.zeros((128, 128), F32)
    coarse_cols = jnp.zeros((128, 128), F32)
    for x in range(ROWS):
        end = rows[x][:, 384:512].astype(F32)
        both = jnp.concatenate([pltpu.roll(end, x + 1, 1), pltpu.roll(end, x + 2, 1)], axis=0)
        skip_cols = jnp.where(lane == x, both, skip_cols)
    for i in range(ROWS // 2):
        end = coarse_rows[i][:, 128:256].astype(F32)
        coarse_cols = jnp.where(lane == i, pltpu.roll(end, i + 1, 1), coarse_cols)
    piece = jnp.concatenate([skip_cols.T[:16], coarse_cols.T[:16]], axis=0).astype(BF)
    col_ref[...] = piece
    send_ref[31] = piece

    @pl.when(tile == last_tile)
    def _():
        skip_t[...] = jnp.zeros_like(skip_t)
        coarse_t[...] = jnp.zeros_like(coarse_t)
        both = jnp.concatenate([rows[15], rows[14]], axis=0).astype(F32)
        for q in range(4):
            skip_t[8 + 128 * q : 136 + 128 * q, :] = both[:, 128 * q : 128 * q + 128].T
        below = coarse_rows[7].astype(F32)
        for q in range(2):
            coarse_t[8 + 128 * q : 136 + 128 * q, :] = below[:, 128 * q : 128 * q + 128].T
        for j in range(32):
            part = jnp.concatenate(
                [
                    skip_t[16 * j + 6 : 16 * j + 26, :],
                    coarse_t[8 * j + 7 : 8 * j + 19, :],
                ],
                axis=0,
            ).astype(BF)
            if j < 31:
                send_ref[j] = part
            else:
                row_ref[...] = part

    @pl.when(tile != last_tile)
    def _():
        row_ref[...] = jnp.zeros_like(row_ref)


def inner_kernel(coarse_ref, skip_ref, up_w_ref, w_ref, bias_ref, first_ref, part_ref, edge_ref, last_ref):
    last_tile = lax.axis_size("tile") - 1
    bottom = lax.axis_index("tile") == last_tile
    rows = jnp.swapaxes(skip_ref[0], 0, 1)
    coarse_rows = jnp.swapaxes(coarse_ref[0], 0, 1)
    up_w = up_rows(up_w_ref)
    up_bias = wide(bias_ref[0], 4)
    first_bias = wide(bias_ref[1], 4)
    by_row = [row_taps(w_ref, r) for r in range(3)]
    weight = jnp.concatenate(by_row, axis=0)
    turned = jnp.where(bottom, turned_taps(w_ref, 0), by_row[0])
    last_weight = jnp.concatenate([turned, by_row[1], by_row[2]], axis=0)
    lane = lanes_of((128, 128))
    lane64 = lanes_of((64, 128))
    ends = jnp.zeros((128, 128), F32)
    last = jnp.zeros((64, 128), F32)
    before = [None, None]
    for k in range(ROWS // 2):
        fine = dot(up_w, spread(coarse_rows[k].astype(F32)))
        for a in range(2):
            i = 2 * k + a
            upsampled = (fine[64 * a : 64 * a + 64] + up_bias).astype(BF)
            row = jnp.concatenate([upsampled, rows[i]], axis=0)
            end = row[:, 384:512].astype(F32)
            ends = jnp.where(lane == i + 2, pltpu.roll(end, i + 3, 1), ends)
            summed = dot(last_weight if i == ROWS - 1 else weight, taps(row))
            low, mid, high = summed[:64], summed[64:128], summed[128:]
            done = high if before[0] is None else before[0] + high
            before = [mid if before[1] is None else before[1] + mid, low]
            if i == 0:
                part_ref[0, 0] = done
            elif i == 1:
                part_ref[0, 1] = done
            else:
                value = done + first_bias
                first_ref[0, i - 1] = silu(value).astype(BF)
                last = jnp.where(lane64 == i + 1, pltpu.roll(value[:, 384:512], i + 2, 1), last)
    part_ref[0, 2] = before[0]
    part_ref[0, 3] = before[1]
    edge_ref[0] = ends
    last_ref[0] = last


def edge_kernel(
    target_ref, first_ref, part_ref, edge_ref, last_ref, above_ref, below_ref, recv_ref, col1_ref, col2_ref,
    row1_ref, up_w_ref, w1_ref, w2_ref, head_ref, bias_ref, head_bias_ref, mask_ref,
    flux_ref, send_ref, halo_skip, halo_coarse, blocks, piece_ref,
):
    member = pl.program_id(0)
    last_tile = lax.axis_size("tile") - 1
    tile = lax.axis_index("tile")
    bottom = tile == last_tile
    top = tile == 0
    lane = lanes_of((128, 128))
    lane64 = lanes_of((64, 128))
    base = member * 32

    @pl.when(jnp.logical_not(bottom))
    def _():
        halo_skip[0] = below_ref[0, 0].astype(F32)
        halo_skip[1] = below_ref[0, 1].astype(F32)
        both = below_ref[0, 2].astype(F32)
        halo_coarse[...] = jnp.concatenate([both[:, :256], both[:, 256:]], axis=0)
        piece_ref[...] = recv_ref[31, pl.ds(pl.multiple_of(base, 32), 32), :].astype(F32)

    @pl.when(bottom)
    def _():
        pieces = [recv_ref[j, pl.ds(pl.multiple_of(base, 32), 32), :].astype(F32) for j in range(31)]
        pieces.append(col1_ref[pl.ds(pl.multiple_of(base, 32), 32), :].astype(F32))
        for q in range(4):
            stacked = jnp.concatenate([pieces[8 * q + j][:16] for j in range(8)], axis=0).T
            halo_skip[0, :, 128 * q : 128 * q + 128] = stacked[:64]
            halo_skip[1, :, 128 * q : 128 * q + 128] = stacked[64:]
        for q in range(2):
            stacked = jnp.concatenate([pieces[16 * q + j][16:24] for j in range(16)], axis=0).T
            halo_coarse[:, 128 * q : 128 * q + 128] = stacked
        piece_ref[...] = row1_ref[pl.ds(pl.multiple_of(base, 32), 32), :].astype(F32)

    up_bias = bias_ref[0]
    up_bias_wide = wide(up_bias, 4)
    first_bias = bias_ref[1]
    first_bias_wide = wide(first_bias, 4)
    second_bias_wide = wide(bias_ref[2], 4)
    head_bias = wide(head_bias_ref[...], 4)

    up_w = up_rows(up_w_ref)
    both = above_ref[0, 2].astype(F32)
    fine = dot(up_w, spread(jnp.concatenate([both[:, :256], both[:, 256:]], axis=0)))
    above = []
    for a in range(2):
        upsampled = (fine[64 * a : 64 * a + 64] + up_bias_wide).astype(BF)
        row = jnp.concatenate([upsampled, above_ref[0, a]], axis=0)
        above.append(jnp.where(top, jnp.zeros_like(row), row))
    turned_up = jnp.concatenate(
        [jnp.concatenate([up_w_ref[0, 1 - q], up_w_ref[1, 1 - q]], axis=1) for q in range(2)], axis=0
    )
    fine = dot(jnp.where(bottom, turned_up, up_w), spread(halo_coarse[...]))
    below = []
    for a in range(2):
        upsampled = (fine[64 * a : 64 * a + 64] + up_bias_wide).astype(BF)
        below.append(jnp.concatenate([upsampled, halo_skip[a].astype(BF)], axis=0))

    pixel = tile * ROWS - 2 + lane
    piece = jnp.concatenate([piece_ref[...], jnp.zeros((96, 128), F32)], axis=0).T
    doubled = jnp.take_along_axis(piece, jnp.minimum(20 + lane // 2, 127), axis=1)
    even = lane % 2 == 0
    zero = jnp.zeros((128, 128), F32)
    spread_piece = jnp.concatenate(
        [jnp.where(even, doubled, zero), jnp.where(even, zero, doubled)], axis=0
    ).astype(BF)
    ghost_up = jnp.concatenate(
        [jnp.concatenate([up_w_ref[1 - q, 0], up_w_ref[1 - q, 1]], axis=1) for q in range(2)], axis=0
    )
    ghost_fine = dot(ghost_up, spread_piece)
    inside = (lane < 20) & (pixel >= 0) & (pixel < COLS)
    ghost = []
    for q in range(2):
        upsampled = (ghost_fine[64 * q : 64 * q + 64] + up_bias).astype(BF).astype(F32)
        column = jnp.concatenate([upsampled, piece[64 * q : 64 * q + 64]], axis=0)
        ghost.append(jnp.where(inside, column, zero))

    corner = jnp.concatenate(
        [col2_ref[pl.ds(pl.multiple_of(base, 32), 32), :].astype(F32), jnp.zeros((96, 128), F32)], axis=0
    ).T
    corner_bf = corner.astype(BF)

    def corner_column(a, e, q, x):
        upsampled = (dot(up_w_ref[a, e], corner_bf) + up_bias).astype(BF).astype(F32)
        column = jnp.concatenate(
            [pltpu.roll(upsampled, 123, 1), pltpu.roll(corner[64 * q : 64 * q + 64], 18 - x, 1)], axis=0
        )
        return jnp.where((lane == 18) & bottom, column, zero)

    corner0 = corner_column(1, 1, 0, 15)
    corner1 = corner_column(1, 0, 1, 15)
    corner2 = corner_column(0, 1, 0, 14)

    ghost_bf = ghost[0].astype(BF)
    around = jnp.concatenate(
        [pltpu.roll(ghost_bf, 1, 1), ghost_bf, pltpu.roll(ghost_bf, 127, 1)], axis=0
    )
    weight = jnp.concatenate([w1_ref[r, 2] for r in range(3)], axis=1)
    added = dot(weight, around)
    weight = jnp.concatenate([w1_ref[2, 1], w1_ref[2, 0]], axis=1)
    added_bottom = dot(weight, jnp.concatenate([corner0, corner2], axis=0).astype(BF))
    added = jnp.where((lane64 == 18) & bottom, added_bottom, added)

    edge = edge_ref[0]
    for x, row in ((0, above[0]), (1, above[1]), (18, below[0]), (19, below[1])):
        end = pltpu.roll(row[:, 384:512].astype(F32), (x + 1) % 128, 1)
        edge = jnp.where(lane == x, end, edge)
    edge = jnp.where((lane == 18) & bottom, zero, edge)
    columns = [edge.astype(BF), (ghost[0] + corner0).astype(BF), (ghost[1] + corner1).astype(BF)]
    around = jnp.concatenate(
        [part for column in columns for part in (pltpu.roll(column, 1, 1), column, pltpu.roll(column, 127, 1))],
        axis=0,
    )
    weight = jnp.concatenate([w1_ref[2 - s, r] for s in range(3) for r in range(3)], axis=1)
    pixel64 = tile * ROWS - 2 + lane64
    inside64 = (lane64 >= 1) & (lane64 <= 18) & (pixel64 >= 0) & (pixel64 < COLS)
    first_ghost = jnp.where(inside64, silu(dot(weight, around) + first_bias), jnp.zeros((64, 128), F32))
    first_ghost = first_ghost.astype(BF).astype(F32)

    by_row = [row_taps(w1_ref, r) for r in range(3)]
    turned = [jnp.where(bottom, turned_taps(w1_ref, r), by_row[r]) for r in range(3)]
    term = dot(by_row[0], taps(above[0]))
    terms = dot(jnp.concatenate([by_row[1], by_row[0]], axis=0), taps(above[1]))
    row_m1 = part_ref[0, 0] + term + terms[:64]
    row_0 = part_ref[0, 1] + terms[64:]
    term = dot(turned[2], taps(below[1]))
    terms = dot(jnp.concatenate([turned[1], by_row[2]], axis=0), taps(below[0]))
    row_15 = part_ref[0, 2] + terms[64:]
    row_16 = part_ref[0, 3] + term + terms[:64]

    def finished(summed, x):
        end = summed[:, 384:512] + jnp.where(lane64 == 127, pltpu.roll(added, 125 - x, 1), 0.0)
        summed = jnp.concatenate([summed[:, :384], end], axis=1)
        return silu(summed + first_bias_wide).astype(BF)

    row_m1 = finished(row_m1, -1)
    outer = {
        -1: jnp.where(top, jnp.zeros_like(row_m1), row_m1),
        0: finished(row_0, 0),
        15: finished(row_15, 15),
        16: finished(row_16, 16),
    }
    last = silu(last_ref[0] + added).astype(BF).astype(F32)

    weight = jnp.concatenate([row_taps(w2_ref, r) for r in range(3)], axis=0)
    head = head_ref[...]
    before = [None, None]
    lane512 = lanes_of((64, COLS))
    for x in range(-1, ROWS + 1):
        if x in outer:
            row = outer[x]
        else:
            row = first_ref[0, x]
            end = jnp.where(lane64 == 127, pltpu.roll(last, 125 - x, 1).astype(BF), row[:, 384:512])
            row = jnp.concatenate([row[:, :384], end], axis=1)
        moved = pltpu.roll(row, COLS - 1, 1)
        end = jnp.where(lane64 == 127, pltpu.roll(first_ghost, 125 - x, 1).astype(BF), moved[:, 384:512])
        after = jnp.concatenate([moved[:, :384], end], axis=1)
        first_part = jnp.where(lane512 == 0, jnp.zeros_like(row), pltpu.roll(row, 1, 1))
        summed = dot(weight, jnp.concatenate([first_part, row, after], axis=0))
        low, mid, high = summed[:64], summed[64:128], summed[128:]
        done = high if before[0] is None else before[0] + high
        before = [mid if before[1] is None else before[1] + mid, low]
        n = x - 1
        if n >= 0:
            second = silu(done + second_bias_wide).astype(BF)
            flux = dot(head, second) + head_bias
            flux_ref[0, :, n, :] = flux
            masked = flux * mask_ref[n : n + 1, :].astype(F32)
            for q in range(COLS // BLOCK):
                blocks[4 * n + q, pl.ds(pl.multiple_of(member * 8, 8), 8), :] = masked[:, 128 * q : 128 * q + 128]

    @pl.when(member == pl.num_programs(0) - 1)
    def _():
        send_ref[...] = jnp.full(send_ref.shape, -1, BF)

        def place(n, carry):
            target = target_ref[n]

            @pl.when(target >= 0)
            def _():
                owner = lax.div(target, CAP)
                slot = (target - owner * CAP).astype(F32)
                send_ref[owner] = jnp.concatenate(
                    [blocks[n], jnp.full((8, 128), slot, F32)], axis=0
                ).astype(BF)

            return carry

        lax.fori_loop(0, target_ref.shape[0], place, 0)


def unpack_kernel(slot_ref, recv_ref, out_ref):
    def place(n, carry):
        slot = slot_ref[n]

        @pl.when(slot >= 0)
        def _():
            out_ref[slot] = recv_ref[n].astype(F32)[:24]

        return carry

    lax.fori_loop(0, slot_ref.shape[0], place, 0)


def whole(shape):
    return pl.BlockSpec(shape, lambda b: (0,) * len(shape))


def member(shape):
    return pl.BlockSpec((1,) + shape, lambda b: (b,) + (0,) * len(shape))


def shards(
    coarse_features,
    skip_features,
    up_weight,
    up_bias,
    first_weight,
    first_bias,
    second_weight,
    second_bias,
    head_weight,
    head_bias,
    land_mask,
    block_target,
):
    faces = lax.axis_size("face")
    tiles = lax.axis_size("tile")
    devices = faces * tiles
    params = pltpu.CompilerParams(vmem_limit_bytes=VMEM_LIMIT)
    sds = jax.ShapeDtypeStruct

    to_up, to_down, send, col, row = pl.pallas_call(
        pack_kernel,
        grid=(3,),
        in_specs=[member((128, 8, 256)), member((64, 16, 512))],
        out_specs=[
            member((3, 64, 512)),
            member((3, 64, 512)),
            pl.BlockSpec((32, 32, 128), lambda b: (0, b, 0)),
            pl.BlockSpec((32, 128), lambda b: (b, 0)),
            pl.BlockSpec((32, 128), lambda b: (b, 0)),
        ],
        out_shape=[
            sds((3, 3, 64, 512), BF),
            sds((3, 3, 64, 512), BF),
            sds((32, 96, 128), BF),
            sds((96, 128), BF),
            sds((96, 128), BF),
        ],
        scratch_shapes=[pltpu.VMEM((544, 128), F32), pltpu.VMEM((272, 128), F32)],
        compiler_params=params,
        name="pack_edges",
    )(coarse_features, skip_features)

    above = lax.ppermute(to_down, "tile", [(t, t + 1) for t in range(tiles - 1)])
    below = lax.ppermute(to_up, "tile", [(t + 1, t) for t in range(tiles - 1)])
    last = tiles - 1

    def around(step):
        return [(f * tiles + last, ((f + step) % faces) * tiles + last) for f in range(faces)]

    both = ("face", "tile")
    col1 = lax.ppermute(col, both, around(1))
    col2 = lax.ppermute(col, both, around(2))
    row1 = lax.ppermute(row, both, around(faces - 1))
    groups = [
        [f * tiles + t for t in range(last)] + [((f + 1) % faces) * tiles + last] for f in range(faces)
    ]
    recv = lax.all_to_all(send, both, 0, 0, axis_index_groups=groups, tiled=True)

    biases = jnp.broadcast_to(jnp.stack([up_bias, first_bias, second_bias])[:, :, None], (3, 64, 128))
    head_biases = jnp.broadcast_to(head_bias[:, None], (8, 128))

    first, parts, edge, last_col = pl.pallas_call(
        inner_kernel,
        grid=(3,),
        in_specs=[
            member((128, 8, 256)),
            member((64, 16, 512)),
            whole((2, 2, 64, 128)),
            whole((3, 3, 64, 128)),
            whole((3, 64, 128)),
        ],
        out_specs=[member((16, 64, 512)), member((4, 64, 512)), member((128, 128)), member((64, 128))],
        out_shape=[
            sds((3, 16, 64, 512), BF),
            sds((3, 4, 64, 512), F32),
            sds((3, 128, 128), F32),
            sds((3, 64, 128), F32),
        ],
        compiler_params=params,
        cost_estimate=pl.CostEstimate(flops=8 * 10**9, bytes_accessed=9 * 10**6, transcendentals=0),
        name="inner_rows",
    )(coarse_features, skip_features, up_weight, first_weight, biases)

    flux, send = pl.pallas_call(
        edge_kernel,
        grid=(3,),
        in_specs=[
            pl.BlockSpec(memory_space=pltpu.SMEM),
            member((16, 64, 512)),
            member((4, 64, 512)),
            member((128, 128)),
            member((64, 128)),
            member((3, 64, 512)),
            member((3, 64, 512)),
            whole((32, 96, 128)),
            whole((96, 128)),
            whole((96, 128)),
            whole((96, 128)),
            whole((2, 2, 64, 128)),
            whole((3, 3, 64, 128)),
            whole((3, 3, 64, 64)),
            whole((8, 64)),
            whole((3, 64, 128)),
            whole((8, 128)),
            whole((16, 512)),
        ],
        out_specs=[member((8, 16, 512)), whole((128, 32, 128))],
        out_shape=[sds((3, 8, 16, 512), F32), sds((devices, 32, 128), BF)],
        scratch_shapes=[
            pltpu.VMEM((2, 64, 512), F32),
            pltpu.VMEM((128, 256), F32),
            pltpu.VMEM((64, 24, 128), F32),
            pltpu.VMEM((32, 128), F32),
        ],
        compiler_params=params,
        name="edges_and_second",
    )(
        block_target, first, parts, edge, last_col, above, below, recv, col1, col2, row1,
        up_weight, first_weight, second_weight, head_weight, biases, head_biases, land_mask,
    )

    got = lax.all_to_all(send, both, 0, 0, tiled=True)
    slots = got[:, 24, 0].astype(jnp.int32)
    ocean = pl.pallas_call(
        unpack_kernel,
        in_specs=[pl.BlockSpec(memory_space=pltpu.SMEM), pl.BlockSpec(memory_space=pltpu.VMEM)],
        out_specs=pl.BlockSpec(memory_space=pltpu.VMEM),
        out_shape=sds((CAP, 24, 128), F32),
        compiler_params=params,
        name="ocean_slots",
    )(slots, got)
    return flux, ocean.reshape(CAP, 3, 8, 128)


def solution(mesh):
    placed = (
        P(None, None, ("face", "tile"), None),
        P(None, None, ("face", "tile"), None),
        P(),
        P(),
        P(),
        P(),
        P(),
        P(),
        P(),
        P(),
        P(("face", "tile"), None),
        P(("face", "tile")),
    )
    return jax.shard_map(
        shards,
        mesh=mesh,
        in_specs=placed,
        out_specs=(P(None, None, ("face", "tile"), None), P(("face", "tile"), None, None, None)),
        check_vma=False,
    )
```

```python
import jax
import jax.numpy as jnp
from jax import lax
from jax.experimental import pallas as pl
from jax.experimental.pallas import tpu as pltpu
from jax.sharding import PartitionSpec as P

BF = jnp.bfloat16
F32 = jnp.float32
ROWS = 16
COLS = 512
BLOCK = 128
CAP = 44
VMEM_LIMIT = 58 * 1024 * 1024
UNPACK_LIMIT = 16 * 1024 * 1024


def dot(a, b):
    return jnp.dot(a, b, preferred_element_type=F32)


def silu(v):
    half = 0.5 * v
    return half * jnp.tanh(half) + half


def lanes_of(shape):
    return lax.broadcasted_iota(jnp.int32, shape, len(shape) - 1)


def wide(column, tiles):
    return jnp.concatenate([column] * tiles, axis=1)


def taps(row):
    lane = lanes_of(row.shape)
    zero = jnp.zeros_like(row)
    before = jnp.where(lane == 0, zero, pltpu.roll(row, 1, 1))
    after = jnp.where(lane == COLS - 1, zero, pltpu.roll(row, COLS - 1, 1))
    return jnp.concatenate([before, row, after], axis=0)


def spread(coarse):
    lane = lanes_of((128, 128))
    parts = [
        jnp.take_along_axis(coarse[:, 128 * p : 128 * p + 128], lane // 2 + 64 * h, axis=1)
        for p in range(2)
        for h in range(2)
    ]
    even = lane % 2 == 0
    zero = jnp.zeros((128, 128), F32)
    top = jnp.concatenate([jnp.where(even, part, zero) for part in parts], axis=1)
    low = jnp.concatenate([jnp.where(even, zero, part) for part in parts], axis=1)
    return jnp.concatenate([top, low], axis=0).astype(BF)


def up_rows(up_ref):
    return jnp.concatenate(
        [jnp.concatenate([up_ref[a, 0], up_ref[a, 1]], axis=1) for a in range(2)], axis=0
    )


def row_taps(weight_ref, r):
    return jnp.concatenate([weight_ref[r, s] for s in range(3)], axis=1)


def turned_taps(weight_ref, r):
    return jnp.concatenate([weight_ref[s, 2 - r] for s in range(3)], axis=1)


def bias_column(row_ref, height):
    return jnp.broadcast_to(row_ref[...], (128, height)).T


def begin(copies):
    for copy in copies:
        copy.start()


def finish(copies):
    for copy in copies:
        copy.wait()


def pack_kernel(
    coarse_hbm, skip_hbm, one_hbm, two_hbm, send_hbm, col_ref, edge_ref,
    coarse_ref, skip_ref, one_ref, two_ref, send_ref, skip_t, coarse_t, sems,
):
    tile = lax.axis_index("tile")
    bottom = tile == lax.axis_size("tile") - 1
    even = lax.rem(tile, 2) == 0

    def loads(member):
        return [
            pltpu.make_async_copy(skip_hbm.at[member], skip_ref.at[member], sems.at[0, member]),
            pltpu.make_async_copy(coarse_hbm.at[member], coarse_ref.at[member], sems.at[1, member]),
        ]

    def store_one(member):
        return [pltpu.make_async_copy(one_ref.at[member], one_hbm.at[member], sems.at[2, member])]

    for member in range(3):
        begin(loads(member))

    def one(member, carry):
        finish(loads(member))
        pack_member(
            member, bottom, even, coarse_ref, skip_ref, one_ref, two_ref, send_ref, col_ref, edge_ref, skip_t, coarse_t
        )

        begin(store_one(member))
        return carry

    lax.fori_loop(0, 3, one, 0)

    @pl.when(bottom)
    def _():
        two_ref[:, 0, :, :128] = edge_ref[...].reshape(3, 64, 128)

    store_two = pltpu.make_async_copy(two_ref, two_hbm, sems.at[3, 0])
    store_two.start()
    ends = pltpu.make_async_copy(send_ref.at[31], send_hbm.at[31], sems.at[4, 0])
    rest = pltpu.make_async_copy(send_ref.at[pl.ds(0, 31)], send_hbm.at[pl.ds(0, 31)], sems.at[4, 1])
    ends.start()

    @pl.when(bottom)
    def _():
        rest.start()

    for member in range(3):
        finish(store_one(member))
    store_two.wait()
    ends.wait()

    @pl.when(bottom)
    def _():
        rest.wait()


def pack_member(
    member, bottom, even, coarse_ref, skip_ref, one_ref, two_ref, send_ref, col_ref, edge_ref, skip_t, coarse_t
):
    own = pl.ds(pl.multiple_of(member * 32, 32), 32)
    rows = jnp.swapaxes(skip_ref[member], 0, 1)
    coarse_rows = jnp.swapaxes(coarse_ref[member], 0, 1)

    def pair(row):
        return jnp.concatenate([row[:64], row[64:]], axis=1)

    top = (rows[0], rows[1], pair(coarse_rows[0]))
    low = (rows[14], rows[15], pair(coarse_rows[7]))
    for k in range(3):
        one_ref[member, k] = jnp.where(even, low[k], top[k])
        two_ref[member, k] = jnp.where(even, top[k], low[k])

    lane = lanes_of((128, 128))
    skip_cols = jnp.zeros((128, 128), F32)
    coarse_cols = jnp.zeros((128, 128), F32)
    for x in range(ROWS):
        end = rows[x][:, 384:512].astype(F32)
        both = jnp.concatenate([pltpu.roll(end, x + 1, 1), pltpu.roll(end, x + 2, 1)], axis=0)
        skip_cols = jnp.where(lane == x, both, skip_cols)
    for i in range(ROWS // 2):
        end = coarse_rows[i][:, 128:256].astype(F32)
        coarse_cols = jnp.where(lane == i, pltpu.roll(end, i + 1, 1), coarse_cols)
    piece = jnp.concatenate([skip_cols.T[:16], coarse_cols.T[:16]], axis=0).astype(BF)
    col_ref[own, :] = piece
    edge_ref[own, :] = piece
    send_ref[31, own, :] = piece

    @pl.when(bottom)
    def _():
        skip_t[...] = jnp.zeros_like(skip_t)
        coarse_t[...] = jnp.zeros_like(coarse_t)
        both = jnp.concatenate([rows[15], rows[14]], axis=0).astype(F32)
        for q in range(4):
            skip_t[8 + 128 * q : 136 + 128 * q, :] = both[:, 128 * q : 128 * q + 128].T
        below = coarse_rows[7].astype(F32)
        for q in range(2):
            coarse_t[8 + 128 * q : 136 + 128 * q, :] = below[:, 128 * q : 128 * q + 128].T
        for j in range(32):
            part = jnp.concatenate(
                [
                    skip_t[16 * j + 6 : 16 * j + 26, :],
                    coarse_t[8 * j + 7 : 8 * j + 19, :],
                ],
                axis=0,
            ).astype(BF)
            if j < 31:
                send_ref[j, own, :] = part
            else:
                edge_ref[pl.ds(pl.multiple_of(96 + member * 32, 32), 32), :] = part


def inner_kernel(
    coarse_hbm, skip_hbm, up_w_hbm, w_hbm, up_bias_hbm, first_bias_hbm, first_hbm, part_hbm, cols_hbm,
    coarse_ref, skip_ref, up_w_ref, w_ref, up_bias_ref, first_bias_ref, first_ref, part_ref, cols_ref, rows_ref, sems,
):
    bottom = lax.axis_index("tile") == lax.axis_size("tile") - 1

    def loads(member):
        return [
            pltpu.make_async_copy(skip_hbm.at[member], skip_ref.at[member], sems.at[0, member]),
            pltpu.make_async_copy(coarse_hbm.at[member], coarse_ref.at[member], sems.at[1, member]),
        ]

    def stores(member):
        return [
            pltpu.make_async_copy(first_ref.at[member], first_hbm.at[member], sems.at[2, member]),
            pltpu.make_async_copy(part_ref.at[member], part_hbm.at[member], sems.at[3, member]),
        ]

    small = [
        pltpu.make_async_copy(source, target, sems.at[5, k])
        for k, (source, target) in enumerate(
            [
                (up_w_hbm, up_w_ref),
                (w_hbm, w_ref),
                (up_bias_hbm, up_bias_ref),
                (first_bias_hbm, first_bias_ref),
            ]
        )
    ]
    begin(small)
    begin(loads(0))
    finish(small)
    up_w = up_rows(up_w_ref)
    up_bias = wide(bias_column(up_bias_ref, 64), 4)
    first_bias = wide(bias_column(first_bias_ref, 64), 4)
    by_row = [row_taps(w_ref, r) for r in range(3)]
    weight = jnp.concatenate(by_row, axis=0)
    turned = jnp.where(bottom, turned_taps(w_ref, 0), by_row[0])
    last_weight = jnp.concatenate([turned, by_row[1], by_row[2]], axis=0)
    cols_ref[...] = jnp.zeros_like(cols_ref)

    def one(member, carry):
        finish(loads(member))

        @pl.when(member < 2)
        def _():
            begin(loads(member + 1))

        rows = jnp.swapaxes(skip_ref[member], 0, 1)
        coarse_rows = jnp.swapaxes(coarse_ref[member], 0, 1)
        lane = lanes_of((128, 128))
        lane64 = lanes_of((64, 128))
        ends = jnp.zeros((128, 128), F32)
        last = jnp.zeros((64, 128), F32)
        before = [None, None]
        for k in range(ROWS // 2):
            fine = dot(up_w, spread(coarse_rows[k].astype(F32)))
            for a in range(2):
                i = 2 * k + a
                upsampled = (fine[64 * a : 64 * a + 64] + up_bias).astype(BF)
                row = jnp.concatenate([upsampled, rows[i]], axis=0)
                rows_ref[i] = row
                end = row[:, 384:512].astype(F32)
                ends = jnp.where(lane == i + 2, pltpu.roll(end, i + 3, 1), ends)
        for k in range(ROWS // 2):
            for a in range(2):
                i = 2 * k + a
                row = rows_ref[i]
                summed = dot(last_weight if i == ROWS - 1 else weight, taps(row))
                low, mid, high = summed[:64], summed[64:128], summed[128:]
                done = high if before[0] is None else before[0] + high
                before = [mid if before[1] is None else before[1] + mid, low]
                if i == 0:
                    part_ref[member, 0] = done
                elif i == 1:
                    part_ref[member, 1] = done
                else:
                    value = done + first_bias
                    first_ref[member, i - 1] = silu(value).astype(BF)
                    last = jnp.where(lane64 == i + 1, pltpu.roll(value[:, 384:512], i + 2, 1), last)
        part_ref[member, 2] = before[0]
        part_ref[member, 3] = before[1]
        shift = member * 32
        cols_ref[:128] = cols_ref[:128] + pltpu.roll(ends, shift, 1)
        cols_ref[128:] = cols_ref[128:] + pltpu.roll(last, shift, 1)
        begin(stores(member))
        return carry

    lax.fori_loop(0, 3, one, 0)
    cols = pltpu.make_async_copy(cols_ref, cols_hbm, sems.at[4, 0])
    cols.start()
    for member in range(3):
        finish(stores(member))
    cols.wait()


def edge_kernel(
    first_hbm, part_hbm, cols_hbm, one_ref, two_ref, recv_ref, far_ref, across_ref,
    up_w_hbm, w1_hbm, w2_hbm, head_hbm, up_bias_hbm, first_bias_hbm, second_bias_hbm, head_bias_hbm, mask_hbm,
    target_hbm, flux_ref, send_ref,
    first_ref, part_ref, cols_ref, up_w_ref, w1_ref, w2_ref, head_ref, up_bias_ref, first_bias_ref,
    second_bias_ref, head_bias_ref, mask_ref, target_ref, halo_skip, halo_coarse, piece_ref, rows_ref, second_ref, sems,
):
    tile = lax.axis_index("tile")
    bottom = tile == lax.axis_size("tile") - 1
    top = tile == 0
    even_tile = lax.rem(tile, 2) == 0
    even_face = lax.rem(lax.axis_index("face"), 2) == 0

    def loads(member):
        return [
            pltpu.make_async_copy(first_hbm.at[member], first_ref.at[member], sems.at[0, member]),
            pltpu.make_async_copy(part_hbm.at[member], part_ref.at[member], sems.at[1, member]),
        ]

    small = [
        pltpu.make_async_copy(source, target, sems.at[2, k])
        for k, (source, target) in enumerate(
            [
                (up_w_hbm, up_w_ref),
                (w1_hbm, w1_ref),
                (w2_hbm, w2_ref),
                (head_hbm, head_ref),
                (up_bias_hbm, up_bias_ref),
                (first_bias_hbm, first_bias_ref),
                (second_bias_hbm, second_bias_ref),
                (head_bias_hbm, head_bias_ref),
                (mask_hbm, mask_ref),
                (target_hbm, target_ref),
                (cols_hbm, cols_ref),
            ]
        )
    ]
    begin(small)
    for member in range(3):
        begin(loads(member))

    @pl.when(jnp.logical_not(bottom))
    def _():
        for member in range(3):
            for a in range(2):
                halo_skip[member, a] = jnp.where(even_tile, one_ref[member, a], two_ref[member, a])
            both = jnp.where(even_tile, one_ref[member, 2], two_ref[member, 2]).astype(F32)
            halo_coarse[member] = jnp.concatenate([both[:, :256], both[:, 256:]], axis=0)
        piece_ref[...] = recv_ref[31].astype(F32)

    @pl.when(bottom)
    def _():
        near, far = two_ref[:, 0, :, :128].reshape(192, 128), far_ref[...]
        from_previous = jnp.where(even_face, far[:96], near[:96])
        for member in range(3):
            own = slice(32 * member, 32 * member + 32)
            pieces = [recv_ref[j].astype(F32)[own] for j in range(31)]
            pieces.append(from_previous.astype(F32)[own])
            for q in range(4):
                stacked = jnp.concatenate([pieces[8 * q + j][:16] for j in range(8)], axis=0).T.astype(BF)
                halo_skip[member, 0, :, 128 * q : 128 * q + 128] = stacked[:64]
                halo_skip[member, 1, :, 128 * q : 128 * q + 128] = stacked[64:]
            for q in range(2):
                stacked = jnp.concatenate([pieces[16 * q + j][16:24] for j in range(16)], axis=0).T
                halo_coarse[member, :, 128 * q : 128 * q + 128] = stacked
        piece_ref[...] = jnp.where(even_face, near[96:], far[96:]).astype(F32)

    finish(small)
    up_bias = bias_column(up_bias_ref, 64)
    up_bias_wide = wide(up_bias, 4)
    first_bias = bias_column(first_bias_ref, 64)
    first_bias_wide = wide(first_bias, 4)
    second_bias_wide = wide(bias_column(second_bias_ref, 64), 4)
    head_bias = wide(bias_column(head_bias_ref, 8), 4)
    lane = lanes_of((128, 128))
    place = lax.rem(lane, 32)
    lane64 = lanes_of((64, 128))
    place64 = lax.rem(lane64, 32)
    zero = jnp.zeros((128, 128), F32)
    ghost_rows = jnp.zeros((32, 128), F32)

    up_w = up_rows(up_w_ref)
    turned_up = jnp.concatenate(
        [jnp.concatenate([up_w_ref[0, 1 - q], up_w_ref[1, 1 - q]], axis=1) for q in range(2)], axis=0
    )
    below_w = jnp.where(bottom, turned_up, up_w)
    edge = cols_ref[:128]
    for member in range(3):
        both = jnp.where(even_tile, two_ref[member, 2], one_ref[member, 2]).astype(F32)
        fine = dot(up_w, spread(jnp.concatenate([both[:, :256], both[:, 256:]], axis=0)))
        fine_below = dot(below_w, spread(halo_coarse[member]))
        for a in range(2):
            upsampled = (fine[64 * a : 64 * a + 64] + up_bias_wide).astype(BF)
            skip = jnp.where(even_tile, two_ref[member, a], one_ref[member, a])
            row = jnp.concatenate([upsampled, skip], axis=0)
            row = jnp.where(top, jnp.zeros_like(row), row)
            upsampled = (fine_below[64 * a : 64 * a + 64] + up_bias_wide).astype(BF)
            row_below = jnp.concatenate([upsampled, halo_skip[member, a]], axis=0)
            for x, value in ((a, row), (18 + a, row_below)):
                rows_ref[member, a if x < 2 else 2 + a] = value
                end = pltpu.roll(value[:, 384:512].astype(F32), (32 * member + x + 1) % 128, 1)
                edge = jnp.where(lane == 32 * member + x, end, edge)

    pixel = tile * ROWS - 2 + place
    piece = jnp.concatenate([piece_ref[...], ghost_rows], axis=0).T
    doubled = jnp.take_along_axis(piece, jnp.minimum(lane - place + 20 + lax.div(place, 2), 127), axis=1)
    even = lax.rem(lane, 2) == 0
    spread_piece = jnp.concatenate(
        [jnp.where(even, doubled, zero), jnp.where(even, zero, doubled)], axis=0
    ).astype(BF)
    ghost_up = jnp.concatenate(
        [jnp.concatenate([up_w_ref[1 - q, 0], up_w_ref[1 - q, 1]], axis=1) for q in range(2)], axis=0
    )
    ghost_fine = dot(ghost_up, spread_piece)
    inside = (place < 20) & (pixel >= 0) & (pixel < COLS) & (lane < 96)
    ghost = []
    for q in range(2):
        upsampled = (ghost_fine[64 * q : 64 * q + 64] + up_bias).astype(BF).astype(F32)
        joined = jnp.concatenate([upsampled, piece[64 * q : 64 * q + 64]], axis=0)
        ghost.append(jnp.where(inside, joined, zero))

    corner = jnp.concatenate([across_ref[...].astype(F32), ghost_rows], axis=0).T
    at_corner = dot(
        jnp.concatenate([up_w_ref[1, 1], up_w_ref[1, 0], up_w_ref[0, 1]], axis=0), corner.astype(BF)
    )
    held = (place == 18) & bottom & (lane < 96)

    def corner_column(k, q, x):
        upsampled = (at_corner[64 * k : 64 * k + 64] + up_bias).astype(BF).astype(F32)
        joined = jnp.concatenate(
            [pltpu.roll(upsampled, 123, 1), pltpu.roll(corner[64 * q : 64 * q + 64], 18 - x, 1)], axis=0
        )
        return jnp.where(held, joined, zero)

    corner0 = corner_column(0, 0, 15)
    corner1 = corner_column(1, 1, 15)
    corner2 = corner_column(2, 0, 14)

    def around(joined):
        return [pltpu.roll(joined, 1, 1), joined, pltpu.roll(joined, 127, 1)]

    weight = jnp.concatenate([w1_ref[r, 2] for r in range(3)], axis=1)
    added = dot(weight, jnp.concatenate(around(ghost[0].astype(BF)), axis=0))
    weight = jnp.concatenate([w1_ref[2, 1], w1_ref[2, 0]], axis=1)
    added_bottom = dot(weight, jnp.concatenate([corner0, corner2], axis=0).astype(BF))
    added = jnp.where((place64 == 18) & bottom, added_bottom, added)

    edge = jnp.where((place == 18) & bottom, zero, edge)
    columns = [edge.astype(BF), (ghost[0] + corner0).astype(BF), (ghost[1] + corner1).astype(BF)]
    weight = jnp.concatenate([w1_ref[2 - s, r] for s in range(3) for r in range(3)], axis=1)
    summed = dot(weight, jnp.concatenate([part for joined in columns for part in around(joined)], axis=0))
    pixel64 = tile * ROWS - 2 + place64
    inside64 = (place64 >= 1) & (place64 <= 18) & (pixel64 >= 0) & (pixel64 < COLS)
    first_ghost = jnp.where(inside64, silu(summed + first_bias), jnp.zeros((64, 128), F32))
    last = silu(cols_ref[128:] + added)

    by_row = [row_taps(w1_ref, r) for r in range(3)]
    turned = [jnp.where(bottom, turned_taps(w1_ref, r), by_row[r]) for r in range(3)]
    second_weight = jnp.concatenate([row_taps(w2_ref, r) for r in range(3)], axis=0)
    head = head_ref[...]
    lane512 = lanes_of((64, COLS))

    def one(member, carry):
        base = 125 - 32 * member

        def finished(summed, x):
            end = summed[:, 384:512] + jnp.where(lane64 == 127, pltpu.roll(added, base - x, 1), 0.0)
            summed = jnp.concatenate([summed[:, :384], end], axis=1)
            return silu(summed + first_bias_wide).astype(BF)

        finish(loads(member))
        term = dot(by_row[0], taps(rows_ref[member, 0]))
        terms = dot(jnp.concatenate([by_row[1], by_row[0]], axis=0), taps(rows_ref[member, 1]))
        row_m1 = finished(part_ref[member, 0] + term + terms[:64], -1)
        row_0 = finished(part_ref[member, 1] + terms[64:], 0)
        term = dot(turned[2], taps(rows_ref[member, 3]))
        terms = dot(jnp.concatenate([turned[1], by_row[2]], axis=0), taps(rows_ref[member, 2]))
        row_15 = finished(part_ref[member, 2] + terms[64:], 15)
        row_16 = finished(part_ref[member, 3] + term + terms[:64], 16)
        outer = {-1: jnp.where(top, jnp.zeros_like(row_m1), row_m1), 0: row_0, 15: row_15, 16: row_16}

        before = [None, None]
        for x in range(-1, ROWS + 1):
            if x in outer:
                row = outer[x]
            else:
                row = first_ref[member, x]
                end = jnp.where(lane64 == 127, pltpu.roll(last, base - x, 1).astype(BF), row[:, 384:512])
                row = jnp.concatenate([row[:, :384], end], axis=1)
            moved = pltpu.roll(row, COLS - 1, 1)
            end = jnp.where(
                lane64 == 127, pltpu.roll(first_ghost, base - x, 1).astype(BF), moved[:, 384:512]
            )
            after = jnp.concatenate([moved[:, :384], end], axis=1)
            first_part = jnp.where(lane512 == 0, jnp.zeros_like(row), pltpu.roll(row, 1, 1))
            summed = dot(second_weight, jnp.concatenate([first_part, row, after], axis=0))
            low, mid, high = summed[:64], summed[64:128], summed[128:]
            done = high if before[0] is None else before[0] + high
            before = [mid if before[1] is None else before[1] + mid, low]
            n = x - 1
            if n >= 0:
                second_ref[n] = silu(done + second_bias_wide).astype(BF)
        for n in range(ROWS):
            flux_ref[member, :, n, :] = dot(head, second_ref[n]) + head_bias
        return carry

    lax.fori_loop(0, 3, one, 0)

    target = target_ref[...]
    owner = jnp.where(target >= 0, lax.div(jnp.maximum(target, 0), CAP), -1)
    slot = jnp.where(target >= 0, target - owner * CAP + 1, 0)
    wanted = lax.broadcasted_iota(jnp.int32, (128, 64), 0)
    by_pixel_row = jnp.where(jnp.broadcast_to(owner, (128, 64)) == wanted, 1.0, 0.0).astype(BF)
    block = lax.broadcasted_iota(jnp.int32, (64, 64), 0)
    place = lax.broadcasted_iota(jnp.int32, (64, 64), 1)
    moved = jnp.where(block == 4 * lax.rem(place, 16) + lax.div(place, 16), 1.0, 0.0).astype(BF)
    chosen = dot(by_pixel_row, moved).astype(BF)
    mask = mask_ref[...].astype(F32)
    packed = []
    for member in range(3):
        for k in range(8):
            masked = (flux_ref[member, k] * mask).astype(BF)
            blocks = jnp.concatenate([masked[:, 128 * q : 128 * q + 128] for q in range(4)], axis=0)
            packed.append(dot(chosen, blocks).astype(BF))
    slots = jnp.broadcast_to(slot.astype(F32), (128, 64)).astype(BF)
    slots = jnp.sum(by_pixel_row.astype(F32) * slots.astype(F32), axis=1, keepdims=True)
    slots = jnp.broadcast_to(slots, (128, 128)).astype(BF)
    packed += [slots] * 8
    send_ref[...] = jnp.swapaxes(jnp.stack(packed, axis=0), 0, 1)


def unpack_kernel(recv_ref, out_ref):
    rows = jnp.swapaxes(recv_ref[...], 0, 1)
    slots = rows[24].astype(F32).T[:48]
    wanted = (lax.broadcasted_iota(jnp.int32, slots.shape, 0) + 1).astype(F32)
    chosen = jnp.where(slots == wanted, 1.0, 0.0).astype(BF)
    for k in range(24):
        out_ref[:, k, :] = dot(chosen, rows[k])[:CAP]


def vmem(count):
    return [pl.BlockSpec(memory_space=pltpu.VMEM)] * count


def hbm(count):
    return [pl.BlockSpec(memory_space=pltpu.HBM)] * count


def shards(
    coarse_features,
    skip_features,
    up_weight,
    up_bias,
    first_weight,
    first_bias,
    second_weight,
    second_bias,
    head_weight,
    head_bias,
    land_mask,
    block_target,
):
    faces = lax.axis_size("face")
    tiles = lax.axis_size("tile")
    devices = faces * tiles
    params = pltpu.CompilerParams(vmem_limit_bytes=VMEM_LIMIT)
    sds = jax.ShapeDtypeStruct

    one, two, send, col, edges = pl.pallas_call(
        pack_kernel,
        in_specs=hbm(2),
        out_specs=hbm(3) + vmem(2),
        out_shape=[
            sds((3, 3, 64, 512), BF),
            sds((3, 3, 64, 512), BF),
            sds((32, 96, 128), BF),
            sds((96, 128), BF),
            sds((192, 128), BF),
        ],
        scratch_shapes=[
            pltpu.VMEM((3, 128, 8, 256), BF),
            pltpu.VMEM((3, 64, 16, 512), BF),
            pltpu.VMEM((3, 3, 64, 512), BF),
            pltpu.VMEM((3, 3, 64, 512), BF),
            pltpu.VMEM((32, 96, 128), BF),
            pltpu.VMEM((544, 128), F32),
            pltpu.VMEM((272, 128), F32),
            pltpu.SemaphoreType.DMA((5, 3)),
        ],
        compiler_params=params,
        name="pack_edges",
    )(coarse_features, skip_features)

    last = tiles - 1

    both = ("face", "tile")

    def swapped(bits):
        return [(f * tiles + last, (f ^ bits) * tiles + last) for f in range(faces)]

    strips = [f * tiles for f in range(faces)]
    first_pairs = [(s + t, s + (t ^ 1)) for s in strips for t in range(tiles)]
    second_pairs = [(s + t, s + ((t - 1) ^ 1) + 1) for s in strips for t in range(1, last)]
    got_one = lax.ppermute(one, both, first_pairs)
    got_two = lax.ppermute(two, both, second_pairs + swapped(1))
    far = lax.ppermute(edges, both, swapped(3))
    across = lax.ppermute(col, both, swapped(2))
    groups = [
        [f * tiles + t for t in range(last)] + [((f + 1) % faces) * tiles + last] for f in range(faces)
    ]
    recv = lax.all_to_all(send, both, 0, 0, axis_index_groups=groups, tiled=True)

    up_bias, first_bias, second_bias = (b.reshape(1, 64) for b in (up_bias, first_bias, second_bias))
    first, parts, cols = pl.pallas_call(
        inner_kernel,
        in_specs=hbm(6),
        out_specs=hbm(3),
        out_shape=[sds((3, 16, 64, 512), BF), sds((3, 4, 64, 512), F32), sds((192, 128), F32)],
        scratch_shapes=[
            pltpu.VMEM((3, 128, 8, 256), BF),
            pltpu.VMEM((3, 64, 16, 512), BF),
            pltpu.VMEM((2, 2, 64, 128), BF),
            pltpu.VMEM((3, 3, 64, 128), BF),
            pltpu.VMEM((1, 64), F32),
            pltpu.VMEM((1, 64), F32),
            pltpu.VMEM((3, 16, 64, 512), BF),
            pltpu.VMEM((3, 4, 64, 512), F32),
            pltpu.VMEM((192, 128), F32),
            pltpu.VMEM((16, 128, 512), BF),
            pltpu.SemaphoreType.DMA((6, 4)),
        ],
        compiler_params=params,
        name="inner_rows",
    )(coarse_features, skip_features, up_weight, first_weight, up_bias, first_bias)

    flux, send = pl.pallas_call(
        edge_kernel,
        in_specs=hbm(3) + vmem(5) + hbm(10),
        out_specs=vmem(2),
        out_shape=[sds((3, 8, 16, 512), F32), sds((devices, 32, 128), BF)],
        scratch_shapes=[
            pltpu.VMEM((3, 16, 64, 512), BF),
            pltpu.VMEM((3, 4, 64, 512), F32),
            pltpu.VMEM((192, 128), F32),
            pltpu.VMEM((2, 2, 64, 128), BF),
            pltpu.VMEM((3, 3, 64, 128), BF),
            pltpu.VMEM((3, 3, 64, 64), BF),
            pltpu.VMEM((8, 64), BF),
            pltpu.VMEM((1, 64), F32),
            pltpu.VMEM((1, 64), F32),
            pltpu.VMEM((1, 64), F32),
            pltpu.VMEM((1, 8), F32),
            pltpu.VMEM((16, 512), jnp.int32),
            pltpu.VMEM((1, 64), jnp.int32),
            pltpu.VMEM((3, 2, 64, 512), BF),
            pltpu.VMEM((3, 128, 256), F32),
            pltpu.VMEM((96, 128), F32),
            pltpu.VMEM((3, 4, 128, 512), BF),
            pltpu.VMEM((16, 64, 512), BF),
            pltpu.SemaphoreType.DMA((3, 11)),
        ],
        compiler_params=params,
        name="edges_and_second",
    )(
        first, parts, cols, got_one, got_two, recv, far, across,
        up_weight, first_weight, second_weight, head_weight, up_bias, first_bias, second_bias,
        head_bias.reshape(1, 8), land_mask, block_target.reshape(1, 64),
    )

    got = lax.all_to_all(send, both, 0, 0, tiled=True)
    ocean = pl.pallas_call(
        unpack_kernel,
        in_specs=vmem(1),
        out_specs=vmem(1)[0],
        out_shape=sds((CAP, 24, 128), F32),
        compiler_params=pltpu.CompilerParams(vmem_limit_bytes=UNPACK_LIMIT),
        name="ocean_slots",
    )(got)
    return flux, ocean.reshape(CAP, 3, 8, 128)


def solution(mesh):
    placed = (
        P(None, None, ("face", "tile"), None),
        P(None, None, ("face", "tile"), None),
        P(),
        P(),
        P(),
        P(),
        P(),
        P(),
        P(),
        P(),
        P(("face", "tile"), None),
        P(("face", "tile")),
    )
    return jax.shard_map(
        shards,
        mesh=mesh,
        in_specs=placed,
        out_specs=(P(None, None, ("face", "tile"), None), P(("face", "tile"), None, None, None)),
        check_vma=False,
    )
```

```python
import jax
import jax.numpy as jnp
from jax import lax
from jax.experimental import pallas as pl
from jax.experimental.pallas import tpu as pltpu
from jax.sharding import PartitionSpec as P

BF = jnp.bfloat16
F32 = jnp.float32
ROWS = 16
COLS = 512
BLOCK = 128
CAP = 44
VMEM_LIMIT = 58 * 1024 * 1024
UNPACK_LIMIT = 16 * 1024 * 1024


def dot(a, b):
    return jnp.dot(a, b, preferred_element_type=F32)


def silu(v):
    half = 0.5 * v
    return half * jnp.tanh(half) + half


def lanes_of(shape):
    return lax.broadcasted_iota(jnp.int32, shape, len(shape) - 1)


def wide(column, tiles):
    return jnp.concatenate([column] * tiles, axis=1)


def taps(row):
    lane = lanes_of(row.shape)
    zero = jnp.zeros_like(row)
    before = jnp.where(lane == 0, zero, pltpu.roll(row, 1, 1))
    after = jnp.where(lane == COLS - 1, zero, pltpu.roll(row, COLS - 1, 1))
    return jnp.concatenate([before, row, after], axis=0)


def spread(coarse):
    lane = lanes_of((128, 128))
    parts = [
        jnp.take_along_axis(coarse[:, 128 * p : 128 * p + 128], lane // 2 + 64 * h, axis=1)
        for p in range(2)
        for h in range(2)
    ]
    even = lane % 2 == 0
    zero = jnp.zeros((128, 128), F32)
    top = jnp.concatenate([jnp.where(even, part, zero) for part in parts], axis=1)
    low = jnp.concatenate([jnp.where(even, zero, part) for part in parts], axis=1)
    return jnp.concatenate([top, low], axis=0).astype(BF)


def up_rows(up_ref):
    return jnp.concatenate(
        [jnp.concatenate([up_ref[a, 0], up_ref[a, 1]], axis=1) for a in range(2)], axis=0
    )


def row_taps(weight_ref, r):
    return jnp.concatenate([weight_ref[r, s] for s in range(3)], axis=1)


def turned_taps(weight_ref, r):
    return jnp.concatenate([weight_ref[s, 2 - r] for s in range(3)], axis=1)


def bias_column(row_ref, height):
    return jnp.broadcast_to(row_ref[...], (128, height)).T


def begin(copies):
    for copy in copies:
        copy.start()


def finish(copies):
    for copy in copies:
        copy.wait()


def pack_kernel(
    coarse_hbm, skip_hbm, up_w_hbm, w_hbm, up_bias_hbm, one_hbm, two_hbm, send_hbm, col_ref, edge_ref,
    coarse_ref, skip_ref, up_w_ref, w_ref, up_bias_ref, one_ref, two_ref, send_ref, skip_t, coarse_t, sems,
):
    tile = lax.axis_index("tile")
    bottom = tile == lax.axis_size("tile") - 1
    even = lax.rem(tile, 2) == 0

    def loads(member):
        return [
            pltpu.make_async_copy(skip_hbm.at[member], skip_ref.at[member], sems.at[0, member]),
            pltpu.make_async_copy(coarse_hbm.at[member], coarse_ref.at[member], sems.at[1, member]),
        ]

    def store_one(member):
        return [pltpu.make_async_copy(one_ref.at[member], one_hbm.at[member], sems.at[2, member])]

    small = [
        pltpu.make_async_copy(up_w_hbm, up_w_ref, sems.at[5, 0]),
        pltpu.make_async_copy(w_hbm, w_ref, sems.at[5, 1]),
        pltpu.make_async_copy(up_bias_hbm, up_bias_ref, sems.at[5, 2]),
    ]
    begin(small)
    for member in range(3):
        begin(loads(member))
    finish(small)
    up_w = up_rows(up_w_ref)
    up_bias = wide(bias_column(up_bias_ref, 64), 4)
    by_row = [row_taps(w_ref, r) for r in range(3)]

    def one(member, carry):
        finish(loads(member))
        pack_member(
            member, bottom, even, up_w, up_bias, by_row,
            coarse_ref, skip_ref, one_ref, two_ref, send_ref, col_ref, edge_ref, skip_t, coarse_t,
        )

        begin(store_one(member))
        return carry

    lax.fori_loop(0, 3, one, 0)

    @pl.when(bottom)
    def _():
        two_ref[:, :, :128] = edge_ref[...].reshape(3, 64, 128)

    store_two = pltpu.make_async_copy(two_ref, two_hbm, sems.at[3, 0])
    store_two.start()
    ends = pltpu.make_async_copy(send_ref.at[31], send_hbm.at[31], sems.at[4, 0])
    rest = pltpu.make_async_copy(send_ref.at[pl.ds(0, 31)], send_hbm.at[pl.ds(0, 31)], sems.at[4, 1])
    ends.start()

    @pl.when(bottom)
    def _():
        rest.start()

    for member in range(3):
        finish(store_one(member))
    store_two.wait()
    ends.wait()

    @pl.when(bottom)
    def _():
        rest.wait()


def pack_member(
    member, bottom, even, up_w, up_bias, by_row,
    coarse_ref, skip_ref, one_ref, two_ref, send_ref, col_ref, edge_ref, skip_t, coarse_t,
):
    own = pl.ds(pl.multiple_of(member * 32, 32), 32)
    rows = jnp.swapaxes(skip_ref[member], 0, 1)
    coarse_rows = jnp.swapaxes(coarse_ref[member], 0, 1)

    def joined(coarse_row, pair):
        fine = dot(up_w, spread(coarse_row.astype(F32)))
        parts = [(fine[64 * a : 64 * a + 64] + up_bias).astype(BF) for a in range(2)]
        return [jnp.concatenate([part, row], axis=0) for part, row in zip(parts, pair)]

    lane64 = lanes_of((64, 128))

    def outgoing(reached, own, pair):
        ends = jnp.zeros((64, 128), F32)
        for a, row in enumerate(pair):
            end = row[:, 384:].astype(F32)
            for h in range(2):
                moved = pltpu.roll(end[64 * h : 64 * h + 64], 2 * a + h + 1, 1)
                ends = jnp.where(lane64 == 2 * a + h, moved, ends)
        return jnp.concatenate([reached, own, ends], axis=1).astype(BF)

    pair = joined(coarse_rows[0], rows[0:2])
    terms = dot(jnp.concatenate([by_row[2], by_row[1]], axis=0), taps(pair[0]))
    top = outgoing(terms[:64], terms[64:] + dot(by_row[2], taps(pair[1])), pair)
    pair = joined(coarse_rows[7], rows[14:16])
    terms = dot(jnp.concatenate([by_row[0], by_row[1]], axis=0), taps(pair[1]))
    low = outgoing(terms[:64], terms[64:] + dot(by_row[0], taps(pair[0])), pair)
    one_ref[member] = jnp.where(even, low, top)
    two_ref[member] = jnp.where(even, top, low)

    lane = lanes_of((128, 128))
    skip_cols = jnp.zeros((128, 128), F32)
    coarse_cols = jnp.zeros((128, 128), F32)
    for x in range(ROWS):
        end = rows[x][:, 384:512].astype(F32)
        both = jnp.concatenate([pltpu.roll(end, x + 1, 1), pltpu.roll(end, x + 2, 1)], axis=0)
        skip_cols = jnp.where(lane == x, both, skip_cols)
    for i in range(ROWS // 2):
        end = coarse_rows[i][:, 128:256].astype(F32)
        coarse_cols = jnp.where(lane == i, pltpu.roll(end, i + 1, 1), coarse_cols)
    piece = jnp.concatenate([skip_cols.T[:16], coarse_cols.T[:16]], axis=0).astype(BF)
    col_ref[own, :] = piece
    edge_ref[own, :] = piece
    send_ref[31, own, :] = piece

    @pl.when(bottom)
    def _():
        skip_t[...] = jnp.zeros_like(skip_t)
        coarse_t[...] = jnp.zeros_like(coarse_t)
        both = jnp.concatenate([rows[15], rows[14]], axis=0).astype(F32)
        for q in range(4):
            skip_t[8 + 128 * q : 136 + 128 * q, :] = both[:, 128 * q : 128 * q + 128].T
        below = coarse_rows[7].astype(F32)
        for q in range(2):
            coarse_t[8 + 128 * q : 136 + 128 * q, :] = below[:, 128 * q : 128 * q + 128].T
        for j in range(32):
            part = jnp.concatenate(
                [
                    skip_t[16 * j + 6 : 16 * j + 26, :],
                    coarse_t[8 * j + 7 : 8 * j + 19, :],
                ],
                axis=0,
            ).astype(BF)
            if j < 31:
                send_ref[j, own, :] = part
            else:
                edge_ref[pl.ds(pl.multiple_of(96 + member * 32, 32), 32), :] = part


def inner_kernel(
    coarse_hbm, skip_hbm, up_w_hbm, w_hbm, up_bias_hbm, first_bias_hbm, first_hbm, part_hbm, cols_hbm,
    coarse_ref, skip_ref, up_w_ref, w_ref, up_bias_ref, first_bias_ref, first_ref, part_ref, cols_ref, rows_ref, sems,
):
    bottom = lax.axis_index("tile") == lax.axis_size("tile") - 1

    def loads(member):
        return [
            pltpu.make_async_copy(skip_hbm.at[member], skip_ref.at[member], sems.at[0, member]),
            pltpu.make_async_copy(coarse_hbm.at[member], coarse_ref.at[member], sems.at[1, member]),
        ]

    def stores(member):
        return [
            pltpu.make_async_copy(first_ref.at[member], first_hbm.at[member], sems.at[2, member]),
            pltpu.make_async_copy(part_ref.at[member], part_hbm.at[member], sems.at[3, member]),
        ]

    small = [
        pltpu.make_async_copy(source, target, sems.at[5, k])
        for k, (source, target) in enumerate(
            [
                (up_w_hbm, up_w_ref),
                (w_hbm, w_ref),
                (up_bias_hbm, up_bias_ref),
                (first_bias_hbm, first_bias_ref),
            ]
        )
    ]
    begin(small)
    begin(loads(0))
    finish(small)
    up_w = up_rows(up_w_ref)
    up_bias = wide(bias_column(up_bias_ref, 64), 4)
    first_bias = wide(bias_column(first_bias_ref, 64), 4)
    by_row = [row_taps(w_ref, r) for r in range(3)]
    weight = jnp.concatenate(by_row, axis=0)
    turned = jnp.where(bottom, turned_taps(w_ref, 0), by_row[0])
    last_weight = jnp.concatenate([turned, by_row[1], by_row[2]], axis=0)
    cols_ref[...] = jnp.zeros_like(cols_ref)

    def one(member, carry):
        finish(loads(member))

        @pl.when(member < 2)
        def _():
            begin(loads(member + 1))

        rows = jnp.swapaxes(skip_ref[member], 0, 1)
        coarse_rows = jnp.swapaxes(coarse_ref[member], 0, 1)
        lane = lanes_of((128, 128))
        lane64 = lanes_of((64, 128))
        ends = jnp.zeros((128, 128), F32)
        last = jnp.zeros((64, 128), F32)
        before = [None, None]
        for k in range(ROWS // 2):
            fine = dot(up_w, spread(coarse_rows[k].astype(F32)))
            for a in range(2):
                i = 2 * k + a
                upsampled = (fine[64 * a : 64 * a + 64] + up_bias).astype(BF)
                row = jnp.concatenate([upsampled, rows[i]], axis=0)
                rows_ref[i] = row
                end = row[:, 384:512].astype(F32)
                ends = jnp.where(lane == i + 2, pltpu.roll(end, i + 3, 1), ends)
        for k in range(ROWS // 2):
            for a in range(2):
                i = 2 * k + a
                row = rows_ref[i]
                summed = dot(last_weight if i == ROWS - 1 else weight, taps(row))
                low, mid, high = summed[:64], summed[64:128], summed[128:]
                done = high if before[0] is None else before[0] + high
                before = [mid if before[1] is None else before[1] + mid, low]
                if i == 0:
                    part_ref[member, 0] = done
                elif i == 1:
                    part_ref[member, 1] = done
                else:
                    value = done + first_bias
                    first_ref[member, i - 1] = silu(value).astype(BF)
                    last = jnp.where(lane64 == i + 1, pltpu.roll(value[:, 384:512], i + 2, 1), last)
        part_ref[member, 2] = before[0]
        part_ref[member, 3] = before[1]
        shift = member * 32
        cols_ref[:128] = cols_ref[:128] + pltpu.roll(ends, shift, 1)
        cols_ref[128:] = cols_ref[128:] + pltpu.roll(last, shift, 1)
        begin(stores(member))
        return carry

    lax.fori_loop(0, 3, one, 0)
    cols = pltpu.make_async_copy(cols_ref, cols_hbm, sems.at[4, 0])
    cols.start()
    for member in range(3):
        finish(stores(member))
    cols.wait()


def edge_kernel(
    first_hbm, part_hbm, cols_hbm, one_hbm, two_hbm, recv_hbm, far_hbm, across_hbm,
    up_w_hbm, w1_hbm, w2_hbm, head_hbm, up_bias_hbm, first_bias_hbm, second_bias_hbm, head_bias_hbm, mask_hbm,
    target_hbm, flux_hbm, send_hbm,
    first_ref, part_ref, cols_ref, up_w_ref, w1_ref, w2_ref, head_ref, up_bias_ref, first_bias_ref,
    second_bias_ref, head_bias_ref, mask_ref, target_ref, terms_ref, ends_ref, piece_ref, second_ref,
    one_ref, two_ref, recv_ref, far_ref, across_ref, flux_ref, send_ref, sems,
):
    tile = lax.axis_index("tile")
    bottom = tile == lax.axis_size("tile") - 1
    top = tile == 0
    even_tile = lax.rem(tile, 2) == 0
    even_face = lax.rem(lax.axis_index("face"), 2) == 0

    def loads(member):
        return [
            pltpu.make_async_copy(first_hbm.at[member], first_ref.at[member], sems.at[0, member]),
            pltpu.make_async_copy(part_hbm.at[member], part_ref.at[member], sems.at[1, member]),
        ]

    small = [
        pltpu.make_async_copy(source, target, sems.at[2, k])
        for k, (source, target) in enumerate(
            [
                (up_w_hbm, up_w_ref),
                (w1_hbm, w1_ref),
                (w2_hbm, w2_ref),
                (head_hbm, head_ref),
                (up_bias_hbm, up_bias_ref),
                (first_bias_hbm, first_bias_ref),
                (second_bias_hbm, second_bias_ref),
                (head_bias_hbm, head_bias_ref),
                (mask_hbm, mask_ref),
                (target_hbm, target_ref),
                (cols_hbm, cols_ref),
                (one_hbm, one_ref),
                (two_hbm, two_ref),
                (across_hbm, across_ref),
                (far_hbm, far_ref),
                (recv_hbm.at[31], recv_ref.at[31]),
            ]
        )
    ]
    chunks = pltpu.make_async_copy(
        recv_hbm.at[pl.ds(0, 31)], recv_ref.at[pl.ds(0, 31)], sems.at[3, 0]
    )

    def store_flux(member):
        return [pltpu.make_async_copy(flux_ref.at[member], flux_hbm.at[member], sems.at[3, 1 + member])]

    @pl.when(bottom)
    def _():
        chunks.start()

    begin(small)
    begin(loads(0))
    finish(small)
    begin(loads(1))
    begin(loads(2))

    @pl.when(bottom)
    def _():
        chunks.wait()

    up_bias = bias_column(up_bias_ref, 64)
    up_bias_wide = wide(up_bias, 4)
    first_bias = bias_column(first_bias_ref, 64)
    first_bias_wide = wide(first_bias, 4)
    second_bias_wide = wide(bias_column(second_bias_ref, 64), 4)
    head_bias = wide(bias_column(head_bias_ref, 8), 4)
    lane = lanes_of((128, 128))
    place = lax.rem(lane, 32)
    lane64 = lanes_of((64, 128))
    place64 = lax.rem(lane64, 32)
    zero = jnp.zeros((128, 128), F32)
    ghost_rows = jnp.zeros((32, 128), F32)

    by_row = [row_taps(w1_ref, r) for r in range(3)]
    above = jnp.where(even_tile, two_ref[...], one_ref[...])

    @pl.when(jnp.logical_not(bottom))
    def _():
        below = jnp.where(even_tile, one_ref[...], two_ref[...]).astype(F32)
        for member in range(3):
            terms_ref[member, 2] = below[member, :, :512]
            terms_ref[member, 3] = below[member, :, 512:1024]
            ends_ref[member] = below[member, :, 1024:]
        piece_ref[...] = recv_ref[31].astype(F32)

    @pl.when(bottom)
    def _():
        near, far = two_ref[:, :, :128].reshape(192, 128), far_ref[...]
        from_previous = jnp.where(even_face, far[:96], near[:96])
        turned_up = jnp.concatenate(
            [jnp.concatenate([up_w_ref[0, 1 - q], up_w_ref[1, 1 - q]], axis=1) for q in range(2)], axis=0
        )
        near_weight = jnp.concatenate([by_row[2], turned_taps(w1_ref, 1)], axis=0)
        far_weight = turned_taps(w1_ref, 2)
        for member in range(3):
            own = slice(32 * member, 32 * member + 32)
            pieces = [recv_ref[j].astype(F32)[own] for j in range(31)]
            pieces.append(from_previous.astype(F32)[own])
            skip = jnp.concatenate(
                [
                    jnp.concatenate([pieces[8 * q + j][:16] for j in range(8)], axis=0).T.astype(BF)
                    for q in range(4)
                ],
                axis=1,
            )
            coarse = jnp.concatenate(
                [
                    jnp.concatenate([pieces[16 * q + j][16:24] for j in range(16)], axis=0).T
                    for q in range(2)
                ],
                axis=1,
            )
            fine = dot(turned_up, spread(coarse))
            beyond = [
                jnp.concatenate(
                    [(fine[64 * a : 64 * a + 64] + up_bias_wide).astype(BF), skip[64 * a : 64 * a + 64]], axis=0
                )
                for a in range(2)
            ]
            terms = dot(near_weight, taps(beyond[0]))
            terms_ref[member, 2] = terms[:64]
            terms_ref[member, 3] = terms[64:] + dot(far_weight, taps(beyond[1]))
            ends_ref[member] = jnp.zeros((64, 128), F32)
        piece_ref[...] = jnp.where(even_face, near[96:], far[96:]).astype(F32)

    edge = cols_ref[:128]
    for member in range(3):
        end = above[member, :, 1024:].astype(F32)
        terms_ref[member, 0] = above[member, :, 512:1024].astype(F32)
        terms_ref[member, 1] = above[member, :, :512].astype(F32)
        for x, ends in ((0, end), (18, ends_ref[member])):
            for a in range(2):
                target = 32 * member + x + a
                moved = jnp.concatenate(
                    [pltpu.roll(ends, (target - 2 * a - h) % 128, 1) for h in range(2)], axis=0
                )
                edge = jnp.where(lane == target, moved, edge)

    pixel = tile * ROWS - 2 + place
    piece = jnp.concatenate([piece_ref[...], ghost_rows], axis=0).T
    doubled = jnp.take_along_axis(piece, jnp.minimum(lane - place + 20 + lax.div(place, 2), 127), axis=1)
    even = lax.rem(lane, 2) == 0
    spread_piece = jnp.concatenate(
        [jnp.where(even, doubled, zero), jnp.where(even, zero, doubled)], axis=0
    ).astype(BF)
    ghost_up = jnp.concatenate(
        [jnp.concatenate([up_w_ref[1 - q, 0], up_w_ref[1 - q, 1]], axis=1) for q in range(2)], axis=0
    )
    ghost_fine = dot(ghost_up, spread_piece)
    inside = (place < 20) & (pixel >= 0) & (pixel < COLS) & (lane < 96)
    ghost = []
    for q in range(2):
        upsampled = (ghost_fine[64 * q : 64 * q + 64] + up_bias).astype(BF).astype(F32)
        joined = jnp.concatenate([upsampled, piece[64 * q : 64 * q + 64]], axis=0)
        ghost.append(jnp.where(inside, joined, zero))

    corner = jnp.concatenate([across_ref[...].astype(F32), ghost_rows], axis=0).T
    at_corner = dot(
        jnp.concatenate([up_w_ref[1, 1], up_w_ref[1, 0], up_w_ref[0, 1]], axis=0), corner.astype(BF)
    )
    held = (place == 18) & bottom & (lane < 96)

    def corner_column(k, q, x):
        upsampled = (at_corner[64 * k : 64 * k + 64] + up_bias).astype(BF).astype(F32)
        joined = jnp.concatenate(
            [pltpu.roll(upsampled, 123, 1), pltpu.roll(corner[64 * q : 64 * q + 64], 18 - x, 1)], axis=0
        )
        return jnp.where(held, joined, zero)

    corner0 = corner_column(0, 0, 15)
    corner1 = corner_column(1, 1, 15)
    corner2 = corner_column(2, 0, 14)

    def around(joined):
        return [pltpu.roll(joined, 1, 1), joined, pltpu.roll(joined, 127, 1)]

    weight = jnp.concatenate([w1_ref[r, 2] for r in range(3)], axis=1)
    added = dot(weight, jnp.concatenate(around(ghost[0].astype(BF)), axis=0))
    weight = jnp.concatenate([w1_ref[2, 1], w1_ref[2, 0]], axis=1)
    added_bottom = dot(weight, jnp.concatenate([corner0, corner2], axis=0).astype(BF))
    added = jnp.where((place64 == 18) & bottom, added_bottom, added)

    edge = jnp.where((place == 18) & bottom, zero, edge)
    columns = [edge.astype(BF), (ghost[0] + corner0).astype(BF), (ghost[1] + corner1).astype(BF)]
    weight = jnp.concatenate([w1_ref[2 - s, r] for s in range(3) for r in range(3)], axis=1)
    summed = dot(weight, jnp.concatenate([part for joined in columns for part in around(joined)], axis=0))
    pixel64 = tile * ROWS - 2 + place64
    inside64 = (place64 >= 1) & (place64 <= 18) & (pixel64 >= 0) & (pixel64 < COLS)
    first_ghost = jnp.where(inside64, silu(summed + first_bias), jnp.zeros((64, 128), F32))
    last = silu(cols_ref[128:] + added)

    second_weight = jnp.concatenate([row_taps(w2_ref, r) for r in range(3)], axis=0)
    head = head_ref[...]
    lane512 = lanes_of((64, COLS))

    def one(member, carry):
        base = 125 - 32 * member

        def finished(summed, x):
            end = summed[:, 384:512] + jnp.where(lane64 == 127, pltpu.roll(added, base - x, 1), 0.0)
            summed = jnp.concatenate([summed[:, :384], end], axis=1)
            return silu(summed + first_bias_wide).astype(BF)

        finish(loads(member))
        row_m1, row_0, row_15, row_16 = (
            finished(part_ref[member, k] + terms_ref[member, k], x) for k, x in enumerate((-1, 0, 15, 16))
        )
        outer = {-1: jnp.where(top, jnp.zeros_like(row_m1), row_m1), 0: row_0, 15: row_15, 16: row_16}

        before = [None, None]
        for x in range(-1, ROWS + 1):
            if x in outer:
                row = outer[x]
            else:
                row = first_ref[member, x]
                end = jnp.where(lane64 == 127, pltpu.roll(last, base - x, 1).astype(BF), row[:, 384:512])
                row = jnp.concatenate([row[:, :384], end], axis=1)
            moved = pltpu.roll(row, COLS - 1, 1)
            end = jnp.where(
                lane64 == 127, pltpu.roll(first_ghost, base - x, 1).astype(BF), moved[:, 384:512]
            )
            after = jnp.concatenate([moved[:, :384], end], axis=1)
            first_part = jnp.where(lane512 == 0, jnp.zeros_like(row), pltpu.roll(row, 1, 1))
            summed = dot(second_weight, jnp.concatenate([first_part, row, after], axis=0))
            low, mid, high = summed[:64], summed[64:128], summed[128:]
            done = high if before[0] is None else before[0] + high
            before = [mid if before[1] is None else before[1] + mid, low]
            n = x - 1
            if n >= 0:
                second_ref[n] = silu(done + second_bias_wide).astype(BF)
        for n in range(ROWS):
            flux_ref[member, :, n, :] = dot(head, second_ref[n]) + head_bias
        begin(store_flux(member))
        return carry

    lax.fori_loop(0, 3, one, 0)

    target = target_ref[...]
    owner = jnp.where(target >= 0, lax.div(jnp.maximum(target, 0), CAP), -1)
    slot = jnp.where(target >= 0, target - owner * CAP + 1, 0)
    wanted = lax.broadcasted_iota(jnp.int32, (128, 64), 0)
    by_pixel_row = jnp.where(jnp.broadcast_to(owner, (128, 64)) == wanted, 1.0, 0.0).astype(BF)
    block = lax.broadcasted_iota(jnp.int32, (64, 64), 0)
    place = lax.broadcasted_iota(jnp.int32, (64, 64), 1)
    moved = jnp.where(block == 4 * lax.rem(place, 16) + lax.div(place, 16), 1.0, 0.0).astype(BF)
    chosen = dot(by_pixel_row, moved).astype(BF)
    mask = mask_ref[...].astype(F32)
    packed = []
    for member in range(3):
        for k in range(8):
            masked = (flux_ref[member, k] * mask).astype(BF)
            blocks = jnp.concatenate([masked[:, 128 * q : 128 * q + 128] for q in range(4)], axis=0)
            packed.append(dot(chosen, blocks).astype(BF))
    slots = jnp.broadcast_to(slot.astype(F32), (128, 64)).astype(BF)
    slots = jnp.sum(by_pixel_row.astype(F32) * slots.astype(F32), axis=1, keepdims=True)
    slots = jnp.broadcast_to(slots, (128, 128)).astype(BF)
    packed += [slots] * 8
    send_ref[...] = jnp.swapaxes(jnp.stack(packed, axis=0), 0, 1)
    send = pltpu.make_async_copy(send_ref, send_hbm, sems.at[3, 4])
    send.start()
    for member in range(3):
        finish(store_flux(member))
    send.wait()


def unpack_kernel(recv_ref, out_ref):
    rows = jnp.swapaxes(recv_ref[...], 0, 1)
    slots = rows[24].astype(F32).T[:48]
    wanted = (lax.broadcasted_iota(jnp.int32, slots.shape, 0) + 1).astype(F32)
    chosen = jnp.where(slots == wanted, 1.0, 0.0).astype(BF)
    for k in range(24):
        out_ref[:, k, :] = dot(chosen, rows[k])[:CAP]


def vmem(count):
    return [pl.BlockSpec(memory_space=pltpu.VMEM)] * count


def hbm(count):
    return [pl.BlockSpec(memory_space=pltpu.HBM)] * count


def shards(
    coarse_features,
    skip_features,
    up_weight,
    up_bias,
    first_weight,
    first_bias,
    second_weight,
    second_bias,
    head_weight,
    head_bias,
    land_mask,
    block_target,
):
    faces = lax.axis_size("face")
    tiles = lax.axis_size("tile")
    devices = faces * tiles
    params = pltpu.CompilerParams(vmem_limit_bytes=VMEM_LIMIT)
    sds = jax.ShapeDtypeStruct

    up_bias, first_bias, second_bias = (b.reshape(1, 64) for b in (up_bias, first_bias, second_bias))
    one, two, send, col, edges = pl.pallas_call(
        pack_kernel,
        in_specs=hbm(5),
        out_specs=hbm(3) + vmem(2),
        out_shape=[
            sds((3, 64, 1152), BF),
            sds((3, 64, 1152), BF),
            sds((32, 96, 128), BF),
            sds((96, 128), BF),
            sds((192, 128), BF),
        ],
        scratch_shapes=[
            pltpu.VMEM((3, 128, 8, 256), BF),
            pltpu.VMEM((3, 64, 16, 512), BF),
            pltpu.VMEM((2, 2, 64, 128), BF),
            pltpu.VMEM((3, 3, 64, 128), BF),
            pltpu.VMEM((1, 64), F32),
            pltpu.VMEM((3, 64, 1152), BF),
            pltpu.VMEM((3, 64, 1152), BF),
            pltpu.VMEM((32, 96, 128), BF),
            pltpu.VMEM((544, 128), F32),
            pltpu.VMEM((272, 128), F32),
            pltpu.SemaphoreType.DMA((6, 3)),
        ],
        compiler_params=params,
        name="pack_edges",
    )(coarse_features, skip_features, up_weight, first_weight, up_bias)

    last = tiles - 1

    both = ("face", "tile")

    def swapped(bits):
        return [(f * tiles + last, (f ^ bits) * tiles + last) for f in range(faces)]

    strips = [f * tiles for f in range(faces)]
    first_pairs = [(s + t, s + (t ^ 1)) for s in strips for t in range(tiles)]
    second_pairs = [(s + t, s + ((t - 1) ^ 1) + 1) for s in strips for t in range(1, last)]
    got_one = lax.ppermute(one, both, first_pairs)
    got_two = lax.ppermute(two, both, second_pairs + swapped(1))
    far = lax.ppermute(edges, both, swapped(3))
    across = lax.ppermute(col, both, swapped(2))
    groups = [
        [f * tiles + t for t in range(last)] + [((f + 1) % faces) * tiles + last] for f in range(faces)
    ]
    recv = lax.all_to_all(send, both, 0, 0, axis_index_groups=groups, tiled=True)

    first, parts, cols = pl.pallas_call(
        inner_kernel,
        in_specs=hbm(6),
        out_specs=hbm(3),
        out_shape=[sds((3, 16, 64, 512), BF), sds((3, 4, 64, 512), F32), sds((192, 128), F32)],
        scratch_shapes=[
            pltpu.VMEM((3, 128, 8, 256), BF),
            pltpu.VMEM((3, 64, 16, 512), BF),
            pltpu.VMEM((2, 2, 64, 128), BF),
            pltpu.VMEM((3, 3, 64, 128), BF),
            pltpu.VMEM((1, 64), F32),
            pltpu.VMEM((1, 64), F32),
            pltpu.VMEM((3, 16, 64, 512), BF),
            pltpu.VMEM((3, 4, 64, 512), F32),
            pltpu.VMEM((192, 128), F32),
            pltpu.VMEM((16, 128, 512), BF),
            pltpu.SemaphoreType.DMA((6, 4)),
        ],
        compiler_params=params,
        name="inner_rows",
    )(coarse_features, skip_features, up_weight, first_weight, up_bias, first_bias)

    flux, send = pl.pallas_call(
        edge_kernel,
        in_specs=hbm(18),
        out_specs=hbm(2),
        out_shape=[sds((3, 8, 16, 512), F32), sds((devices, 32, 128), BF)],
        scratch_shapes=[
            pltpu.VMEM((3, 16, 64, 512), BF),
            pltpu.VMEM((3, 4, 64, 512), F32),
            pltpu.VMEM((192, 128), F32),
            pltpu.VMEM((2, 2, 64, 128), BF),
            pltpu.VMEM((3, 3, 64, 128), BF),
            pltpu.VMEM((3, 3, 64, 64), BF),
            pltpu.VMEM((8, 64), BF),
            pltpu.VMEM((1, 64), F32),
            pltpu.VMEM((1, 64), F32),
            pltpu.VMEM((1, 64), F32),
            pltpu.VMEM((1, 8), F32),
            pltpu.VMEM((16, 512), jnp.int32),
            pltpu.VMEM((1, 64), jnp.int32),
            pltpu.VMEM((3, 4, 64, 512), F32),
            pltpu.VMEM((3, 64, 128), F32),
            pltpu.VMEM((96, 128), F32),
            pltpu.VMEM((16, 64, 512), BF),
            pltpu.VMEM((3, 64, 1152), BF),
            pltpu.VMEM((3, 64, 1152), BF),
            pltpu.VMEM((32, 96, 128), BF),
            pltpu.VMEM((192, 128), BF),
            pltpu.VMEM((96, 128), BF),
            pltpu.VMEM((3, 8, 16, 512), F32),
            pltpu.VMEM((128, 32, 128), BF),
            pltpu.SemaphoreType.DMA((4, 16)),
        ],
        compiler_params=params,
        name="edges_and_second",
    )(
        first, parts, cols, got_one, got_two, recv, far, across,
        up_weight, first_weight, second_weight, head_weight, up_bias, first_bias, second_bias,
        head_bias.reshape(1, 8), land_mask, block_target.reshape(1, 64),
    )

    got = lax.all_to_all(send, both, 0, 0, tiled=True)
    ocean = pl.pallas_call(
        unpack_kernel,
        in_specs=vmem(1),
        out_specs=vmem(1)[0],
        out_shape=sds((CAP, 24, 128), F32),
        compiler_params=pltpu.CompilerParams(vmem_limit_bytes=UNPACK_LIMIT),
        name="ocean_slots",
    )(got)
    return flux, ocean.reshape(CAP, 3, 8, 128)


def solution(mesh):
    placed = (
        P(None, None, ("face", "tile"), None),
        P(None, None, ("face", "tile"), None),
        P(),
        P(),
        P(),
        P(),
        P(),
        P(),
        P(),
        P(),
        P(("face", "tile"), None),
        P(("face", "tile")),
    )
    return jax.shard_map(
        shards,
        mesh=mesh,
        in_specs=placed,
        out_specs=(P(None, None, ("face", "tile"), None), P(("face", "tile"), None, None, None)),
        check_vma=False,
    )
```

```python
import jax
import jax.numpy as jnp
from jax import lax
from jax.experimental import pallas as pl
from jax.experimental.pallas import tpu as pltpu
from jax.sharding import PartitionSpec as P

BF = jnp.bfloat16
F32 = jnp.float32
ROWS = 16
COLS = 512
BLOCK = 128
CAP = 44
VMEM_LIMIT = 58 * 1024 * 1024
UNPACK_LIMIT = 16 * 1024 * 1024


def dot(a, b):
    return jnp.dot(a, b, preferred_element_type=F32)


def silu(v):
    half = 0.5 * v
    return half * jnp.tanh(half) + half


def lanes_of(shape):
    return lax.broadcasted_iota(jnp.int32, shape, len(shape) - 1)


def wide(column, tiles):
    return jnp.concatenate([column] * tiles, axis=1)


def taps(row):
    lane = lanes_of(row.shape)
    zero = jnp.zeros_like(row)
    before = jnp.where(lane == 0, zero, pltpu.roll(row, 1, 1))
    after = jnp.where(lane == COLS - 1, zero, pltpu.roll(row, COLS - 1, 1))
    return jnp.concatenate([before, row, after], axis=0)


def spread(coarse):
    lane = lanes_of((128, 128))
    parts = [
        jnp.take_along_axis(coarse[:, 128 * p : 128 * p + 128], lane // 2 + 64 * h, axis=1)
        for p in range(2)
        for h in range(2)
    ]
    even = lane % 2 == 0
    zero = jnp.zeros((128, 128), F32)
    top = jnp.concatenate([jnp.where(even, part, zero) for part in parts], axis=1)
    low = jnp.concatenate([jnp.where(even, zero, part) for part in parts], axis=1)
    return jnp.concatenate([top, low], axis=0).astype(BF)


def up_rows(up_ref):
    return jnp.concatenate(
        [jnp.concatenate([up_ref[a, 0], up_ref[a, 1]], axis=1) for a in range(2)], axis=0
    )


def row_taps(weight_ref, r):
    return jnp.concatenate([weight_ref[r, s] for s in range(3)], axis=1)


def turned_taps(weight_ref, r):
    return jnp.concatenate([weight_ref[s, 2 - r] for s in range(3)], axis=1)


def bias_column(row_ref, height):
    return jnp.broadcast_to(row_ref[...], (128, height)).T


def begin(copies):
    for copy in copies:
        copy.start()


def finish(copies):
    for copy in copies:
        copy.wait()


def pack_kernel(
    coarse_hbm, skip_hbm, up_w_hbm, w_hbm, up_bias_hbm, one_hbm, two_hbm, send_hbm, col_ref, edge_ref,
    coarse_ref, skip_ref, up_w_ref, w_ref, up_bias_ref, one_ref, two_ref, send_ref, skip_t, coarse_t, sems,
):
    tile = lax.axis_index("tile")
    bottom = tile == lax.axis_size("tile") - 1
    even = lax.rem(tile, 2) == 0

    def loads(member):
        return [
            pltpu.make_async_copy(skip_hbm.at[member], skip_ref.at[member], sems.at[0, member]),
            pltpu.make_async_copy(coarse_hbm.at[member], coarse_ref.at[member], sems.at[1, member]),
        ]

    def stores(member):
        part = pl.ds(8 * member, 8)
        return [
            pltpu.make_async_copy(one_ref.at[part], one_hbm.at[part], sems.at[2, member]),
            pltpu.make_async_copy(two_ref.at[part], two_hbm.at[part], sems.at[3, member]),
        ]

    small = [
        pltpu.make_async_copy(up_w_hbm, up_w_ref, sems.at[5, 0]),
        pltpu.make_async_copy(w_hbm, w_ref, sems.at[5, 1]),
        pltpu.make_async_copy(up_bias_hbm, up_bias_ref, sems.at[5, 2]),
    ]
    begin(small)
    for member in range(3):
        begin(loads(member))
    finish(small)
    up_w = up_rows(up_w_ref)
    up_bias = wide(bias_column(up_bias_ref, 64), 4)
    by_row = [row_taps(w_ref, r) for r in range(3)]

    def one(member, carry):
        finish(loads(member))
        one_ends, two_ends = pack_member(
            member, bottom, even, up_w, up_bias, by_row,
            coarse_ref, skip_ref, one_ref, two_ref, send_ref, col_ref, edge_ref, skip_t, coarse_t,
        )

        @pl.when(member < 2)
        def _():
            begin(stores(member))

        return carry[0] + one_ends, carry[1] + two_ends

    nothing = jnp.zeros((64, 128), F32)
    one_ends, two_ends = lax.fori_loop(0, 3, one, (nothing, nothing))
    one_ref[24] = one_ends.astype(BF)
    two_ref[24] = two_ends.astype(BF)

    @pl.when(bottom)
    def _():
        for k in range(3):
            two_ref[16 + k] = edge_ref[64 * k : 64 * k + 64, :]

    rest_of = pl.ds(16, 9)
    tails = [
        pltpu.make_async_copy(one_ref.at[rest_of], one_hbm.at[rest_of], sems.at[2, 2]),
        pltpu.make_async_copy(two_ref.at[rest_of], two_hbm.at[rest_of], sems.at[3, 2]),
    ]
    begin(tails)
    ends = pltpu.make_async_copy(send_ref.at[31], send_hbm.at[31], sems.at[4, 0])
    rest = pltpu.make_async_copy(send_ref.at[pl.ds(0, 31)], send_hbm.at[pl.ds(0, 31)], sems.at[4, 1])
    ends.start()

    @pl.when(bottom)
    def _():
        rest.start()

    for member in range(2):
        finish(stores(member))
    finish(tails)
    ends.wait()

    @pl.when(bottom)
    def _():
        rest.wait()


def pack_member(
    member, bottom, even, up_w, up_bias, by_row,
    coarse_ref, skip_ref, one_ref, two_ref, send_ref, col_ref, edge_ref, skip_t, coarse_t,
):
    own = pl.ds(pl.multiple_of(member * 32, 32), 32)
    rows = jnp.swapaxes(skip_ref[member], 0, 1)
    coarse_rows = jnp.swapaxes(coarse_ref[member], 0, 1)

    def joined(coarse_row, pair):
        fine = dot(up_w, spread(coarse_row.astype(F32)))
        parts = [(fine[64 * a : 64 * a + 64] + up_bias).astype(BF) for a in range(2)]
        return [jnp.concatenate([part, row], axis=0) for part, row in zip(parts, pair)]

    lane64 = lanes_of((64, 128))

    def outgoing(reached, own, pair):
        ends = jnp.zeros((64, 128), F32)
        for a, row in enumerate(pair):
            end = row[:, 384:].astype(F32)
            for h in range(2):
                moved = pltpu.roll(end[64 * h : 64 * h + 64], 2 * a + h + 1, 1)
                ends = jnp.where(lane64 == 2 * a + h, moved, ends)
        return jnp.concatenate([reached, own], axis=1).astype(BF), pltpu.roll(ends, 4 * member, 1)

    pair = joined(coarse_rows[0], rows[0:2])
    terms = dot(jnp.concatenate([by_row[2], by_row[1]], axis=0), taps(pair[0]))
    top = outgoing(terms[:64], terms[64:] + dot(by_row[2], taps(pair[1])), pair)
    pair = joined(coarse_rows[7], rows[14:16])
    terms = dot(jnp.concatenate([by_row[0], by_row[1]], axis=0), taps(pair[1]))
    low = outgoing(terms[:64], terms[64:] + dot(by_row[0], taps(pair[0])), pair)
    for target, kept in ((one_ref, (low, top)), (two_ref, (top, low))):
        terms = jnp.where(even, kept[0][0], kept[1][0])
        for k in range(8):
            target[8 * member + k] = terms[:, 128 * k : 128 * k + 128]
    one_ends = jnp.where(even, low[1], top[1])
    two_ends = jnp.where(even, top[1], low[1])

    lane = lanes_of((128, 128))
    skip_cols = jnp.zeros((128, 128), F32)
    coarse_cols = jnp.zeros((128, 128), F32)
    for x in range(ROWS):
        end = rows[x][:, 384:512].astype(F32)
        both = jnp.concatenate([pltpu.roll(end, x + 1, 1), pltpu.roll(end, x + 2, 1)], axis=0)
        skip_cols = jnp.where(lane == x, both, skip_cols)
    for i in range(ROWS // 2):
        end = coarse_rows[i][:, 128:256].astype(F32)
        coarse_cols = jnp.where(lane == i, pltpu.roll(end, i + 1, 1), coarse_cols)
    piece = jnp.concatenate([skip_cols.T[:16], coarse_cols.T[:16]], axis=0).astype(BF)
    col_ref[own, :] = piece
    edge_ref[own, :] = piece
    send_ref[31, own, :] = piece

    @pl.when(bottom)
    def _():
        skip_t[...] = jnp.zeros_like(skip_t)
        coarse_t[...] = jnp.zeros_like(coarse_t)
        both = jnp.concatenate([rows[15], rows[14]], axis=0).astype(F32)
        for q in range(4):
            skip_t[8 + 128 * q : 136 + 128 * q, :] = both[:, 128 * q : 128 * q + 128].T
        below = coarse_rows[7].astype(F32)
        for q in range(2):
            coarse_t[8 + 128 * q : 136 + 128 * q, :] = below[:, 128 * q : 128 * q + 128].T
        for j in range(32):
            part = jnp.concatenate(
                [
                    skip_t[16 * j + 6 : 16 * j + 26, :],
                    coarse_t[8 * j + 7 : 8 * j + 19, :],
                ],
                axis=0,
            ).astype(BF)
            if j < 31:
                send_ref[j, own, :] = part
            else:
                edge_ref[pl.ds(pl.multiple_of(96 + member * 32, 32), 32), :] = part

    return one_ends, two_ends


def inner_kernel(
    coarse_hbm, skip_hbm, up_w_hbm, w_hbm, up_bias_hbm, first_bias_hbm, first_hbm, part_hbm, cols_hbm,
    coarse_ref, skip_ref, up_w_ref, w_ref, up_bias_ref, first_bias_ref, first_ref, part_ref, cols_ref, rows_ref, sems,
):
    bottom = lax.axis_index("tile") == lax.axis_size("tile") - 1

    def loads(member):
        return [
            pltpu.make_async_copy(skip_hbm.at[member], skip_ref.at[member], sems.at[0, member]),
            pltpu.make_async_copy(coarse_hbm.at[member], coarse_ref.at[member], sems.at[1, member]),
        ]

    def stores(member):
        return [
            pltpu.make_async_copy(first_ref.at[member], first_hbm.at[member], sems.at[2, member]),
            pltpu.make_async_copy(part_ref.at[member], part_hbm.at[member], sems.at[3, member]),
        ]

    small = [
        pltpu.make_async_copy(source, target, sems.at[5, k])
        for k, (source, target) in enumerate(
            [
                (up_w_hbm, up_w_ref),
                (w_hbm, w_ref),
                (up_bias_hbm, up_bias_ref),
                (first_bias_hbm, first_bias_ref),
            ]
        )
    ]
    begin(small)
    begin(loads(0))
    finish(small)
    up_w = up_rows(up_w_ref)
    up_bias = wide(bias_column(up_bias_ref, 64), 4)
    first_bias = wide(bias_column(first_bias_ref, 64), 4)
    by_row = [row_taps(w_ref, r) for r in range(3)]
    weight = jnp.concatenate(by_row, axis=0)
    turned = jnp.where(bottom, turned_taps(w_ref, 0), by_row[0])
    last_weight = jnp.concatenate([turned, by_row[1], by_row[2]], axis=0)
    cols_ref[...] = jnp.zeros_like(cols_ref)

    def one(member, carry):
        finish(loads(member))

        @pl.when(member < 2)
        def _():
            begin(loads(member + 1))

        rows = jnp.swapaxes(skip_ref[member], 0, 1)
        coarse_rows = jnp.swapaxes(coarse_ref[member], 0, 1)
        lane = lanes_of((128, 128))
        lane64 = lanes_of((64, 128))
        ends = jnp.zeros((128, 128), F32)
        last = jnp.zeros((64, 128), F32)
        before = [None, None]
        for k in range(ROWS // 2):
            fine = dot(up_w, spread(coarse_rows[k].astype(F32)))
            for a in range(2):
                i = 2 * k + a
                upsampled = (fine[64 * a : 64 * a + 64] + up_bias).astype(BF)
                row = jnp.concatenate([upsampled, rows[i]], axis=0)
                rows_ref[i] = row
                end = row[:, 384:512].astype(F32)
                ends = jnp.where(lane == i + 2, pltpu.roll(end, i + 3, 1), ends)
        for k in range(ROWS // 2):
            for a in range(2):
                i = 2 * k + a
                row = rows_ref[i]
                summed = dot(last_weight if i == ROWS - 1 else weight, taps(row))
                low, mid, high = summed[:64], summed[64:128], summed[128:]
                done = high if before[0] is None else before[0] + high
                before = [mid if before[1] is None else before[1] + mid, low]
                if i == 0:
                    part_ref[member, 0] = done
                elif i == 1:
                    part_ref[member, 1] = done
                else:
                    value = done + first_bias
                    first_ref[member, i - 1] = silu(value).astype(BF)
                    last = jnp.where(lane64 == i + 1, pltpu.roll(value[:, 384:512], i + 2, 1), last)
        part_ref[member, 2] = before[0]
        part_ref[member, 3] = before[1]
        shift = member * 32
        cols_ref[:128] = cols_ref[:128] + pltpu.roll(ends, shift, 1)
        cols_ref[128:] = cols_ref[128:] + pltpu.roll(last, shift, 1)
        begin(stores(member))
        return carry

    lax.fori_loop(0, 3, one, 0)
    cols = pltpu.make_async_copy(cols_ref, cols_hbm, sems.at[4, 0])
    cols.start()
    for member in range(3):
        finish(stores(member))
    cols.wait()


def edge_kernel(
    first_hbm, part_hbm, cols_hbm, one_hbm, two_hbm, recv_hbm, far_hbm, across_hbm,
    up_w_hbm, w1_hbm, w2_hbm, head_hbm, up_bias_hbm, first_bias_hbm, second_bias_hbm, head_bias_hbm, mask_hbm,
    target_hbm, flux_hbm, send_hbm,
    first_ref, part_ref, cols_ref, up_w_ref, w1_ref, w2_ref, head_ref, up_bias_ref, first_bias_ref,
    second_bias_ref, head_bias_ref, mask_ref, target_ref, terms_ref, ends_ref, piece_ref, second_ref,
    one_ref, two_ref, recv_ref, far_ref, across_ref, flux_ref, send_ref, sems,
):
    tile = lax.axis_index("tile")
    bottom = tile == lax.axis_size("tile") - 1
    top = tile == 0
    even_tile = lax.rem(tile, 2) == 0
    even_face = lax.rem(lax.axis_index("face"), 2) == 0

    def loads(member):
        return [
            pltpu.make_async_copy(first_hbm.at[member], first_ref.at[member], sems.at[0, member]),
            pltpu.make_async_copy(part_hbm.at[member], part_ref.at[member], sems.at[1, member]),
        ]

    small = [
        pltpu.make_async_copy(source, target, sems.at[2, k])
        for k, (source, target) in enumerate(
            [
                (up_w_hbm, up_w_ref),
                (w1_hbm, w1_ref),
                (w2_hbm, w2_ref),
                (head_hbm, head_ref),
                (up_bias_hbm, up_bias_ref),
                (first_bias_hbm, first_bias_ref),
                (second_bias_hbm, second_bias_ref),
                (head_bias_hbm, head_bias_ref),
                (mask_hbm, mask_ref),
                (target_hbm, target_ref),
                (cols_hbm, cols_ref),
                (one_hbm, one_ref),
                (two_hbm, two_ref),
                (across_hbm, across_ref),
                (far_hbm, far_ref),
                (recv_hbm.at[31], recv_ref.at[31]),
            ]
        )
    ]
    chunks = pltpu.make_async_copy(
        recv_hbm.at[pl.ds(0, 31)], recv_ref.at[pl.ds(0, 31)], sems.at[3, 0]
    )

    def store_flux(member):
        return [pltpu.make_async_copy(flux_ref.at[member], flux_hbm.at[member], sems.at[3, 1 + member])]

    @pl.when(bottom)
    def _():
        chunks.start()

    begin(small)
    begin(loads(0))
    finish(small)
    begin(loads(1))
    begin(loads(2))

    @pl.when(bottom)
    def _():
        chunks.wait()

    up_bias = bias_column(up_bias_ref, 64)
    up_bias_wide = wide(up_bias, 4)
    first_bias = bias_column(first_bias_ref, 64)
    first_bias_wide = wide(first_bias, 4)
    second_bias_wide = wide(bias_column(second_bias_ref, 64), 4)
    head_bias = wide(bias_column(head_bias_ref, 8), 4)
    lane = lanes_of((128, 128))
    place = lax.rem(lane, 32)
    lane64 = lanes_of((64, 128))
    place64 = lax.rem(lane64, 32)
    zero = jnp.zeros((128, 128), F32)
    ghost_rows = jnp.zeros((32, 128), F32)

    by_row = [row_taps(w1_ref, r) for r in range(3)]
    above = jnp.where(even_tile, two_ref[...], one_ref[...])
    above = jnp.where(top, jnp.zeros_like(above), above)

    @pl.when(jnp.logical_not(bottom))
    def _():
        below = jnp.where(even_tile, one_ref[...], two_ref[...]).astype(F32)
        for member in range(3):
            for k in range(4):
                terms_ref[member, 2, :, 128 * k : 128 * k + 128] = below[8 * member + k]
                terms_ref[member, 3, :, 128 * k : 128 * k + 128] = below[8 * member + 4 + k]
            ends_ref[member] = pltpu.roll(below[24], (128 - 4 * member) % 128, 1)
        piece_ref[...] = recv_ref[31].astype(F32)

    @pl.when(bottom)
    def _():
        near, far = two_ref[16:19].reshape(192, 128), far_ref[...]
        from_previous = jnp.where(even_face, far[:96], near[:96])
        turned_up = jnp.concatenate(
            [jnp.concatenate([up_w_ref[0, 1 - q], up_w_ref[1, 1 - q]], axis=1) for q in range(2)], axis=0
        )
        near_weight = jnp.concatenate([by_row[2], turned_taps(w1_ref, 1)], axis=0)
        far_weight = turned_taps(w1_ref, 2)
        for member in range(3):
            own = slice(32 * member, 32 * member + 32)
            pieces = [recv_ref[j].astype(F32)[own] for j in range(31)]
            pieces.append(from_previous.astype(F32)[own])
            skip = jnp.concatenate(
                [
                    jnp.concatenate([pieces[8 * q + j][:16] for j in range(8)], axis=0).T.astype(BF)
                    for q in range(4)
                ],
                axis=1,
            )
            coarse = jnp.concatenate(
                [
                    jnp.concatenate([pieces[16 * q + j][16:24] for j in range(16)], axis=0).T
                    for q in range(2)
                ],
                axis=1,
            )
            fine = dot(turned_up, spread(coarse))
            beyond = [
                jnp.concatenate(
                    [(fine[64 * a : 64 * a + 64] + up_bias_wide).astype(BF), skip[64 * a : 64 * a + 64]], axis=0
                )
                for a in range(2)
            ]
            terms = dot(near_weight, taps(beyond[0]))
            terms_ref[member, 2] = terms[:64]
            terms_ref[member, 3] = terms[64:] + dot(far_weight, taps(beyond[1]))
            ends_ref[member] = jnp.zeros((64, 128), F32)
        piece_ref[...] = jnp.where(even_face, near[96:], far[96:]).astype(F32)

    edge = cols_ref[:128]
    for member in range(3):
        end = pltpu.roll(above[24].astype(F32), (128 - 4 * member) % 128, 1)
        for k in range(4):
            terms_ref[member, 0, :, 128 * k : 128 * k + 128] = above[8 * member + 4 + k].astype(F32)
            terms_ref[member, 1, :, 128 * k : 128 * k + 128] = above[8 * member + k].astype(F32)
        for x, ends in ((0, end), (18, ends_ref[member])):
            for a in range(2):
                target = 32 * member + x + a
                moved = jnp.concatenate(
                    [pltpu.roll(ends, (target - 2 * a - h) % 128, 1) for h in range(2)], axis=0
                )
                edge = jnp.where(lane == target, moved, edge)

    pixel = tile * ROWS - 2 + place
    piece = jnp.concatenate([piece_ref[...], ghost_rows], axis=0).T
    doubled = jnp.take_along_axis(piece, jnp.minimum(lane - place + 20 + lax.div(place, 2), 127), axis=1)
    even = lax.rem(lane, 2) == 0
    spread_piece = jnp.concatenate(
        [jnp.where(even, doubled, zero), jnp.where(even, zero, doubled)], axis=0
    ).astype(BF)
    ghost_up = jnp.concatenate(
        [jnp.concatenate([up_w_ref[1 - q, 0], up_w_ref[1 - q, 1]], axis=1) for q in range(2)], axis=0
    )
    ghost_fine = dot(ghost_up, spread_piece)
    inside = (place < 20) & (pixel >= 0) & (pixel < COLS) & (lane < 96)
    ghost = []
    for q in range(2):
        upsampled = (ghost_fine[64 * q : 64 * q + 64] + up_bias).astype(BF).astype(F32)
        joined = jnp.concatenate([upsampled, piece[64 * q : 64 * q + 64]], axis=0)
        ghost.append(jnp.where(inside, joined, zero))

    corner = jnp.concatenate([across_ref[...].astype(F32), ghost_rows], axis=0).T
    at_corner = dot(
        jnp.concatenate([up_w_ref[1, 1], up_w_ref[1, 0], up_w_ref[0, 1]], axis=0), corner.astype(BF)
    )
    held = (place == 18) & bottom & (lane < 96)

    def corner_column(k, q, x):
        upsampled = (at_corner[64 * k : 64 * k + 64] + up_bias).astype(BF).astype(F32)
        joined = jnp.concatenate(
            [pltpu.roll(upsampled, 123, 1), pltpu.roll(corner[64 * q : 64 * q + 64], 18 - x, 1)], axis=0
        )
        return jnp.where(held, joined, zero)

    corner0 = corner_column(0, 0, 15)
    corner1 = corner_column(1, 1, 15)
    corner2 = corner_column(2, 0, 14)

    def around(joined):
        return [pltpu.roll(joined, 1, 1), joined, pltpu.roll(joined, 127, 1)]

    weight = jnp.concatenate([w1_ref[r, 2] for r in range(3)], axis=1)
    added = dot(weight, jnp.concatenate(around(ghost[0].astype(BF)), axis=0))
    weight = jnp.concatenate([w1_ref[2, 1], w1_ref[2, 0]], axis=1)
    added_bottom = dot(weight, jnp.concatenate([corner0, corner2], axis=0).astype(BF))
    added = jnp.where((place64 == 18) & bottom, added_bottom, added)

    edge = jnp.where((place == 18) & bottom, zero, edge)
    columns = [edge.astype(BF), (ghost[0] + corner0).astype(BF), (ghost[1] + corner1).astype(BF)]
    weight = jnp.concatenate([w1_ref[2 - s, r] for s in range(3) for r in range(3)], axis=1)
    summed = dot(weight, jnp.concatenate([part for joined in columns for part in around(joined)], axis=0))
    pixel64 = tile * ROWS - 2 + place64
    inside64 = (place64 >= 1) & (place64 <= 18) & (pixel64 >= 0) & (pixel64 < COLS)
    first_ghost = jnp.where(inside64, silu(summed + first_bias), jnp.zeros((64, 128), F32))
    last = silu(cols_ref[128:] + added)

    second_weight = jnp.concatenate([row_taps(w2_ref, r) for r in range(3)], axis=0)
    head = head_ref[...]
    lane512 = lanes_of((64, COLS))

    def one(member, carry):
        base = 125 - 32 * member

        def finished(summed, x):
            end = summed[:, 384:512] + jnp.where(lane64 == 127, pltpu.roll(added, base - x, 1), 0.0)
            summed = jnp.concatenate([summed[:, :384], end], axis=1)
            return silu(summed + first_bias_wide).astype(BF)

        finish(loads(member))
        row_m1, row_0, row_15, row_16 = (
            finished(part_ref[member, k] + terms_ref[member, k], x) for k, x in enumerate((-1, 0, 15, 16))
        )
        outer = {-1: jnp.where(top, jnp.zeros_like(row_m1), row_m1), 0: row_0, 15: row_15, 16: row_16}

        before = [None, None]
        for x in range(-1, ROWS + 1):
            if x in outer:
                row = outer[x]
            else:
                row = first_ref[member, x]
                end = jnp.where(lane64 == 127, pltpu.roll(last, base - x, 1).astype(BF), row[:, 384:512])
                row = jnp.concatenate([row[:, :384], end], axis=1)
            moved = pltpu.roll(row, COLS - 1, 1)
            end = jnp.where(
                lane64 == 127, pltpu.roll(first_ghost, base - x, 1).astype(BF), moved[:, 384:512]
            )
            after = jnp.concatenate([moved[:, :384], end], axis=1)
            first_part = jnp.where(lane512 == 0, jnp.zeros_like(row), pltpu.roll(row, 1, 1))
            summed = dot(second_weight, jnp.concatenate([first_part, row, after], axis=0))
            low, mid, high = summed[:64], summed[64:128], summed[128:]
            done = high if before[0] is None else before[0] + high
            before = [mid if before[1] is None else before[1] + mid, low]
            n = x - 1
            if n >= 0:
                second_ref[n] = silu(done + second_bias_wide).astype(BF)
        for n in range(ROWS):
            flux_ref[member, :, n, :] = dot(head, second_ref[n]) + head_bias
        begin(store_flux(member))
        return carry

    lax.fori_loop(0, 3, one, 0)

    target = target_ref[...]
    owner = jnp.where(target >= 0, lax.div(jnp.maximum(target, 0), CAP), -1)
    slot = jnp.where(target >= 0, target - owner * CAP + 1, 0)
    wanted = lax.broadcasted_iota(jnp.int32, (128, 64), 0)
    by_pixel_row = jnp.where(jnp.broadcast_to(owner, (128, 64)) == wanted, 1.0, 0.0).astype(BF)
    block = lax.broadcasted_iota(jnp.int32, (64, 64), 0)
    place = lax.broadcasted_iota(jnp.int32, (64, 64), 1)
    moved = jnp.where(block == 4 * lax.rem(place, 16) + lax.div(place, 16), 1.0, 0.0).astype(BF)
    chosen = dot(by_pixel_row, moved).astype(BF)
    mask = mask_ref[...].astype(F32)
    packed = []
    for member in range(3):
        for k in range(8):
            masked = (flux_ref[member, k] * mask).astype(BF)
            blocks = jnp.concatenate([masked[:, 128 * q : 128 * q + 128] for q in range(4)], axis=0)
            packed.append(dot(chosen, blocks).astype(BF))
    slots = jnp.broadcast_to(slot.astype(F32), (128, 64)).astype(BF)
    slots = jnp.sum(by_pixel_row.astype(F32) * slots.astype(F32), axis=1, keepdims=True)
    slots = jnp.broadcast_to(slots, (128, 128)).astype(BF)
    packed += [slots] * 8
    packed = jnp.stack(packed, axis=0)
    sends = []
    for k in range(2):
        part = slice(64 * k, 64 * k + 64)
        send_ref[part] = jnp.swapaxes(packed[:, part], 0, 1)
        half = pl.ds(64 * k, 64)
        sends.append(pltpu.make_async_copy(send_ref.at[half], send_hbm.at[half], sems.at[3, 4 + k]))
        sends[k].start()
    for member in range(3):
        finish(store_flux(member))
    finish(sends)


def unpack_kernel(recv_ref, out_ref):
    rows = jnp.swapaxes(recv_ref[...], 0, 1)
    slots = rows[24].astype(F32).T[:48]
    wanted = (lax.broadcasted_iota(jnp.int32, slots.shape, 0) + 1).astype(F32)
    chosen = jnp.where(slots == wanted, 1.0, 0.0).astype(BF)
    for k in range(24):
        out_ref[:, k, :] = dot(chosen, rows[k])[:CAP]


def vmem(count):
    return [pl.BlockSpec(memory_space=pltpu.VMEM)] * count


def hbm(count):
    return [pl.BlockSpec(memory_space=pltpu.HBM)] * count


def shards(
    coarse_features,
    skip_features,
    up_weight,
    up_bias,
    first_weight,
    first_bias,
    second_weight,
    second_bias,
    head_weight,
    head_bias,
    land_mask,
    block_target,
):
    faces = lax.axis_size("face")
    tiles = lax.axis_size("tile")
    devices = faces * tiles
    params = pltpu.CompilerParams(vmem_limit_bytes=VMEM_LIMIT)
    sds = jax.ShapeDtypeStruct

    up_bias, first_bias, second_bias = (b.reshape(1, 64) for b in (up_bias, first_bias, second_bias))
    one, two, send, col, edges = pl.pallas_call(
        pack_kernel,
        in_specs=hbm(5),
        out_specs=hbm(3) + vmem(2),
        out_shape=[
            sds((25, 64, 128), BF),
            sds((25, 64, 128), BF),
            sds((32, 96, 128), BF),
            sds((96, 128), BF),
            sds((192, 128), BF),
        ],
        scratch_shapes=[
            pltpu.VMEM((3, 128, 8, 256), BF),
            pltpu.VMEM((3, 64, 16, 512), BF),
            pltpu.VMEM((2, 2, 64, 128), BF),
            pltpu.VMEM((3, 3, 64, 128), BF),
            pltpu.VMEM((1, 64), F32),
            pltpu.VMEM((25, 64, 128), BF),
            pltpu.VMEM((25, 64, 128), BF),
            pltpu.VMEM((32, 96, 128), BF),
            pltpu.VMEM((544, 128), F32),
            pltpu.VMEM((272, 128), F32),
            pltpu.SemaphoreType.DMA((6, 3)),
        ],
        compiler_params=params,
        name="pack_edges",
    )(coarse_features, skip_features, up_weight, first_weight, up_bias)

    last = tiles - 1

    both = ("face", "tile")

    def swapped(bits):
        return [(f * tiles + last, (f ^ bits) * tiles + last) for f in range(faces)]

    strips = [f * tiles for f in range(faces)]
    first_pairs = [(s + t, s + (t ^ 1)) for s in strips for t in range(tiles)]
    second_pairs = [(s + t, s + ((t - 1) ^ 1) + 1) for s in strips for t in range(1, last)]
    got_one = lax.ppermute(one, both, first_pairs)
    got_two = lax.ppermute(two, both, second_pairs + swapped(1) + [(f * tiles, (f ^ 1) * tiles) for f in range(faces)])
    far = lax.ppermute(edges, "face", [(f, f ^ 3) for f in range(faces)])
    across = lax.ppermute(col, "face", [(f, f ^ 2) for f in range(faces)])
    groups = [
        [f * tiles + t for t in range(last)] + [((f + 1) % faces) * tiles + last] for f in range(faces)
    ]
    recv = lax.all_to_all(send, both, 0, 0, axis_index_groups=groups, tiled=True)

    first, parts, cols = pl.pallas_call(
        inner_kernel,
        in_specs=hbm(6),
        out_specs=hbm(3),
        out_shape=[sds((3, 16, 64, 512), BF), sds((3, 4, 64, 512), F32), sds((192, 128), F32)],
        scratch_shapes=[
            pltpu.VMEM((3, 128, 8, 256), BF),
            pltpu.VMEM((3, 64, 16, 512), BF),
            pltpu.VMEM((2, 2, 64, 128), BF),
            pltpu.VMEM((3, 3, 64, 128), BF),
            pltpu.VMEM((1, 64), F32),
            pltpu.VMEM((1, 64), F32),
            pltpu.VMEM((3, 16, 64, 512), BF),
            pltpu.VMEM((3, 4, 64, 512), F32),
            pltpu.VMEM((192, 128), F32),
            pltpu.VMEM((16, 128, 512), BF),
            pltpu.SemaphoreType.DMA((6, 4)),
        ],
        compiler_params=params,
        name="inner_rows",
    )(coarse_features, skip_features, up_weight, first_weight, up_bias, first_bias)

    flux, send = pl.pallas_call(
        edge_kernel,
        in_specs=hbm(18),
        out_specs=hbm(2),
        out_shape=[sds((3, 8, 16, 512), F32), sds((devices, 32, 128), BF)],
        scratch_shapes=[
            pltpu.VMEM((3, 16, 64, 512), BF),
            pltpu.VMEM((3, 4, 64, 512), F32),
            pltpu.VMEM((192, 128), F32),
            pltpu.VMEM((2, 2, 64, 128), BF),
            pltpu.VMEM((3, 3, 64, 128), BF),
            pltpu.VMEM((3, 3, 64, 64), BF),
            pltpu.VMEM((8, 64), BF),
            pltpu.VMEM((1, 64), F32),
            pltpu.VMEM((1, 64), F32),
            pltpu.VMEM((1, 64), F32),
            pltpu.VMEM((1, 8), F32),
            pltpu.VMEM((16, 512), jnp.int32),
            pltpu.VMEM((1, 64), jnp.int32),
            pltpu.VMEM((3, 4, 64, 512), F32),
            pltpu.VMEM((3, 64, 128), F32),
            pltpu.VMEM((96, 128), F32),
            pltpu.VMEM((16, 64, 512), BF),
            pltpu.VMEM((25, 64, 128), BF),
            pltpu.VMEM((25, 64, 128), BF),
            pltpu.VMEM((32, 96, 128), BF),
            pltpu.VMEM((192, 128), BF),
            pltpu.VMEM((96, 128), BF),
            pltpu.VMEM((3, 8, 16, 512), F32),
            pltpu.VMEM((128, 32, 128), BF),
            pltpu.SemaphoreType.DMA((4, 16)),
        ],
        compiler_params=params,
        name="edges_and_second",
    )(
        first, parts, cols, got_one, got_two, recv, far, across,
        up_weight, first_weight, second_weight, head_weight, up_bias, first_bias, second_bias,
        head_bias.reshape(1, 8), land_mask, block_target.reshape(1, 64),
    )

    got = lax.all_to_all(send, both, 0, 0, tiled=True)
    ocean = pl.pallas_call(
        unpack_kernel,
        in_specs=vmem(1),
        out_specs=vmem(1)[0],
        out_shape=sds((CAP, 24, 128), F32),
        compiler_params=pltpu.CompilerParams(vmem_limit_bytes=UNPACK_LIMIT),
        name="ocean_slots",
    )(got)
    return flux, ocean.reshape(CAP, 3, 8, 128)


def solution(mesh):
    placed = (
        P(None, None, ("face", "tile"), None),
        P(None, None, ("face", "tile"), None),
        P(),
        P(),
        P(),
        P(),
        P(),
        P(),
        P(),
        P(),
        P(("face", "tile"), None),
        P(("face", "tile")),
    )
    return jax.shard_map(
        shards,
        mesh=mesh,
        in_specs=placed,
        out_specs=(P(None, None, ("face", "tile"), None), P(("face", "tile"), None, None, None)),
        check_vma=False,
    )
```

```python
import jax
import jax.numpy as jnp
from jax import lax
from jax.experimental import pallas as pl
from jax.experimental.pallas import tpu as pltpu
from jax.sharding import PartitionSpec as P

BF = jnp.bfloat16
F32 = jnp.float32
ROWS = 16
COLS = 512
BLOCK = 128
CAP = 44
VMEM_LIMIT = 58 * 1024 * 1024
UNPACK_LIMIT = 16 * 1024 * 1024


def dot(a, b):
    return jnp.dot(a, b, preferred_element_type=F32)


def silu(v):
    half = 0.5 * v
    return half * jnp.tanh(half) + half


def lanes_of(shape):
    return lax.broadcasted_iota(jnp.int32, shape, len(shape) - 1)


def wide(column, tiles):
    return jnp.concatenate([column] * tiles, axis=1)


def taps(row):
    lane = lanes_of(row.shape)
    zero = jnp.zeros_like(row)
    before = jnp.where(lane == 0, zero, pltpu.roll(row, 1, 1))
    after = jnp.where(lane == COLS - 1, zero, pltpu.roll(row, COLS - 1, 1))
    return jnp.concatenate([before, row, after], axis=0)


def spread(coarse):
    lane = lanes_of((128, 128))
    parts = [
        jnp.take_along_axis(coarse[:, 128 * p : 128 * p + 128], lane // 2 + 64 * h, axis=1)
        for p in range(2)
        for h in range(2)
    ]
    even = lane % 2 == 0
    zero = jnp.zeros((128, 128), F32)
    top = jnp.concatenate([jnp.where(even, part, zero) for part in parts], axis=1)
    low = jnp.concatenate([jnp.where(even, zero, part) for part in parts], axis=1)
    return jnp.concatenate([top, low], axis=0).astype(BF)


def up_rows(up_ref):
    return jnp.concatenate(
        [jnp.concatenate([up_ref[a, 0], up_ref[a, 1]], axis=1) for a in range(2)], axis=0
    )


def row_taps(weight_ref, r):
    return jnp.concatenate([weight_ref[r, s] for s in range(3)], axis=1)


def turned_taps(weight_ref, r):
    return jnp.concatenate([weight_ref[s, 2 - r] for s in range(3)], axis=1)


def bias_column(row_ref, height):
    return jnp.broadcast_to(row_ref[...], (128, height)).T


def begin(copies):
    for copy in copies:
        copy.start()


def finish(copies):
    for copy in copies:
        copy.wait()


def pack_kernel(
    coarse_hbm, skip_hbm, up_w_hbm, w_hbm, up_bias_hbm, one_hbm, two_hbm, send_hbm, col_ref, edge_ref,
    coarse_ref, skip_ref, up_w_ref, w_ref, up_bias_ref, one_ref, two_ref, send_ref, skip_t, coarse_t, sems,
):
    tile = lax.axis_index("tile")
    bottom = tile == lax.axis_size("tile") - 1
    even = lax.rem(tile, 2) == 0

    def loads(member):
        return [
            pltpu.make_async_copy(skip_hbm.at[member], skip_ref.at[member], sems.at[0, member]),
            pltpu.make_async_copy(coarse_hbm.at[member], coarse_ref.at[member], sems.at[1, member]),
        ]

    def stores(member):
        part = pl.ds(8 * member, 8)
        return [
            pltpu.make_async_copy(one_ref.at[part], one_hbm.at[part], sems.at[2, member]),
            pltpu.make_async_copy(two_ref.at[part], two_hbm.at[part], sems.at[3, member]),
        ]

    small = [
        pltpu.make_async_copy(up_w_hbm, up_w_ref, sems.at[5, 0]),
        pltpu.make_async_copy(w_hbm, w_ref, sems.at[5, 1]),
        pltpu.make_async_copy(up_bias_hbm, up_bias_ref, sems.at[5, 2]),
    ]
    begin(small)
    for member in range(3):
        begin(loads(member))
    finish(small)
    up_w = up_rows(up_w_ref)
    up_bias = wide(bias_column(up_bias_ref, 64), 4)
    by_row = [row_taps(w_ref, r) for r in range(3)]

    def one(member, carry):
        finish(loads(member))
        one_ends, two_ends = pack_member(
            member, bottom, even, up_w, up_bias, by_row,
            coarse_ref, skip_ref, one_ref, two_ref, send_ref, col_ref, edge_ref, skip_t, coarse_t,
        )

        @pl.when(member < 2)
        def _():
            begin(stores(member))

        return carry[0] + one_ends, carry[1] + two_ends

    nothing = jnp.zeros((64, 128), F32)
    one_ends, two_ends = lax.fori_loop(0, 3, one, (nothing, nothing))
    one_ref[24] = one_ends.astype(BF)
    two_ref[24] = two_ends.astype(BF)

    @pl.when(bottom)
    def _():
        for k in range(3):
            two_ref[16 + k] = edge_ref[64 * k : 64 * k + 64, :]

    rest_of = pl.ds(16, 9)
    tails = [
        pltpu.make_async_copy(one_ref.at[rest_of], one_hbm.at[rest_of], sems.at[2, 2]),
        pltpu.make_async_copy(two_ref.at[rest_of], two_hbm.at[rest_of], sems.at[3, 2]),
    ]
    begin(tails)
    ends = pltpu.make_async_copy(send_ref.at[31], send_hbm.at[31], sems.at[4, 0])
    rest = pltpu.make_async_copy(send_ref.at[pl.ds(0, 31)], send_hbm.at[pl.ds(0, 31)], sems.at[4, 1])
    ends.start()

    @pl.when(bottom)
    def _():
        rest.start()

    for member in range(2):
        finish(stores(member))
    finish(tails)
    ends.wait()

    @pl.when(bottom)
    def _():
        rest.wait()


def pack_member(
    member, bottom, even, up_w, up_bias, by_row,
    coarse_ref, skip_ref, one_ref, two_ref, send_ref, col_ref, edge_ref, skip_t, coarse_t,
):
    own = pl.ds(pl.multiple_of(member * 32, 32), 32)
    rows = jnp.swapaxes(skip_ref[member], 0, 1)
    coarse_rows = jnp.swapaxes(coarse_ref[member], 0, 1)

    def joined(coarse_row, pair):
        fine = dot(up_w, spread(coarse_row.astype(F32)))
        parts = [(fine[64 * a : 64 * a + 64] + up_bias).astype(BF) for a in range(2)]
        return [jnp.concatenate([part, row], axis=0) for part, row in zip(parts, pair)]

    lane64 = lanes_of((64, 128))

    def outgoing(reached, own, pair):
        ends = jnp.zeros((64, 128), F32)
        for a, row in enumerate(pair):
            end = row[:, 384:].astype(F32)
            for h in range(2):
                moved = pltpu.roll(end[64 * h : 64 * h + 64], 2 * a + h + 1, 1)
                ends = jnp.where(lane64 == 2 * a + h, moved, ends)
        return jnp.concatenate([reached, own], axis=1).astype(BF), pltpu.roll(ends, 4 * member, 1)

    pair = joined(coarse_rows[0], rows[0:2])
    terms = dot(jnp.concatenate([by_row[2], by_row[1]], axis=0), taps(pair[0]))
    top = outgoing(terms[:64], terms[64:] + dot(by_row[2], taps(pair[1])), pair)
    pair = joined(coarse_rows[7], rows[14:16])
    terms = dot(jnp.concatenate([by_row[0], by_row[1]], axis=0), taps(pair[1]))
    low = outgoing(terms[:64], terms[64:] + dot(by_row[0], taps(pair[0])), pair)
    for target, kept in ((one_ref, (low, top)), (two_ref, (top, low))):
        terms = jnp.where(even, kept[0][0], kept[1][0])
        for k in range(8):
            target[8 * member + k] = terms[:, 128 * k : 128 * k + 128]
    one_ends = jnp.where(even, low[1], top[1])
    two_ends = jnp.where(even, top[1], low[1])

    lane = lanes_of((128, 128))
    skip_cols = jnp.zeros((128, 128), F32)
    coarse_cols = jnp.zeros((128, 128), F32)
    for x in range(ROWS):
        end = rows[x][:, 384:512].astype(F32)
        both = jnp.concatenate([pltpu.roll(end, x + 1, 1), pltpu.roll(end, x + 2, 1)], axis=0)
        skip_cols = jnp.where(lane == x, both, skip_cols)
    for i in range(ROWS // 2):
        end = coarse_rows[i][:, 128:256].astype(F32)
        coarse_cols = jnp.where(lane == i, pltpu.roll(end, i + 1, 1), coarse_cols)
    piece = jnp.concatenate([skip_cols.T[:16], coarse_cols.T[:16]], axis=0).astype(BF)
    col_ref[own, :] = piece
    edge_ref[own, :] = piece
    send_ref[31, own, :] = piece

    @pl.when(bottom)
    def _():
        skip_t[...] = jnp.zeros_like(skip_t)
        coarse_t[...] = jnp.zeros_like(coarse_t)
        both = jnp.concatenate([rows[15], rows[14]], axis=0).astype(F32)
        for q in range(4):
            skip_t[8 + 128 * q : 136 + 128 * q, :] = both[:, 128 * q : 128 * q + 128].T
        below = coarse_rows[7].astype(F32)
        for q in range(2):
            coarse_t[8 + 128 * q : 136 + 128 * q, :] = below[:, 128 * q : 128 * q + 128].T
        for j in range(32):
            part = jnp.concatenate(
                [
                    skip_t[16 * j + 6 : 16 * j + 26, :],
                    coarse_t[8 * j + 7 : 8 * j + 19, :],
                ],
                axis=0,
            ).astype(BF)
            if j < 31:
                send_ref[j, own, :] = part
            else:
                edge_ref[pl.ds(pl.multiple_of(96 + member * 32, 32), 32), :] = part

    return one_ends, two_ends


def inner_kernel(
    coarse_hbm, skip_hbm, up_w_hbm, w_hbm, up_bias_hbm, first_bias_hbm, first_hbm, part_hbm, cols_hbm,
    coarse_ref, skip_ref, up_w_ref, w_ref, up_bias_ref, first_bias_ref, first_ref, part_ref, cols_ref, rows_ref, sems,
):
    bottom = lax.axis_index("tile") == lax.axis_size("tile") - 1

    def loads(member):
        return [
            pltpu.make_async_copy(skip_hbm.at[member], skip_ref.at[member], sems.at[0, member]),
            pltpu.make_async_copy(coarse_hbm.at[member], coarse_ref.at[member], sems.at[1, member]),
        ]

    def stores(member):
        return [
            pltpu.make_async_copy(first_ref.at[member], first_hbm.at[member], sems.at[2, member]),
            pltpu.make_async_copy(part_ref.at[member], part_hbm.at[member], sems.at[3, member]),
        ]

    small = [
        pltpu.make_async_copy(source, target, sems.at[5, k])
        for k, (source, target) in enumerate(
            [
                (up_w_hbm, up_w_ref),
                (w_hbm, w_ref),
                (up_bias_hbm, up_bias_ref),
                (first_bias_hbm, first_bias_ref),
            ]
        )
    ]
    begin(small)
    begin(loads(0))
    finish(small)
    up_w = up_rows(up_w_ref)
    up_bias = wide(bias_column(up_bias_ref, 64), 4)
    first_bias = wide(bias_column(first_bias_ref, 64), 4)
    by_row = [row_taps(w_ref, r) for r in range(3)]
    weight = jnp.concatenate(by_row, axis=0)
    turned = jnp.where(bottom, turned_taps(w_ref, 0), by_row[0])
    last_weight = jnp.concatenate([turned, by_row[1], by_row[2]], axis=0)
    cols_ref[...] = jnp.zeros_like(cols_ref)

    def one(member, carry):
        finish(loads(member))

        @pl.when(member < 2)
        def _():
            begin(loads(member + 1))

        rows = jnp.swapaxes(skip_ref[member], 0, 1)
        coarse_rows = jnp.swapaxes(coarse_ref[member], 0, 1)
        lane = lanes_of((128, 128))
        lane64 = lanes_of((64, 128))
        ends = jnp.zeros((128, 128), F32)
        last = jnp.zeros((64, 128), F32)
        before = [None, None]
        for k in range(ROWS // 2):
            fine = dot(up_w, spread(coarse_rows[k].astype(F32)))
            for a in range(2):
                i = 2 * k + a
                upsampled = (fine[64 * a : 64 * a + 64] + up_bias).astype(BF)
                row = jnp.concatenate([upsampled, rows[i]], axis=0)
                rows_ref[i] = row
                end = row[:, 384:512].astype(F32)
                ends = jnp.where(lane == i + 2, pltpu.roll(end, i + 3, 1), ends)
        for k in range(ROWS // 2):
            for a in range(2):
                i = 2 * k + a
                row = rows_ref[i]
                summed = dot(last_weight if i == ROWS - 1 else weight, taps(row))
                low, mid, high = summed[:64], summed[64:128], summed[128:]
                done = high if before[0] is None else before[0] + high
                before = [mid if before[1] is None else before[1] + mid, low]
                if i == 0:
                    part_ref[member, 0] = done
                elif i == 1:
                    part_ref[member, 1] = done
                else:
                    value = done + first_bias
                    first_ref[member, i - 1] = silu(value).astype(BF)
                    last = jnp.where(lane64 == i + 1, pltpu.roll(value[:, 384:512], i + 2, 1), last)
        part_ref[member, 2] = before[0]
        part_ref[member, 3] = before[1]
        shift = member * 32
        cols_ref[:128] = cols_ref[:128] + pltpu.roll(ends, shift, 1)
        cols_ref[128:] = cols_ref[128:] + pltpu.roll(last, shift, 1)
        begin(stores(member))
        return carry

    lax.fori_loop(0, 3, one, 0)
    cols = pltpu.make_async_copy(cols_ref, cols_hbm, sems.at[4, 0])
    cols.start()
    for member in range(3):
        finish(stores(member))
    cols.wait()


def edge_kernel(
    first_hbm, part_hbm, cols_hbm, one_hbm, two_hbm, recv_hbm, far_hbm, across_hbm,
    up_w_hbm, w1_hbm, w2_hbm, head_hbm, up_bias_hbm, first_bias_hbm, second_bias_hbm, head_bias_hbm, mask_hbm,
    target_hbm, flux_hbm, send_hbm,
    first_ref, part_ref, cols_ref, up_w_ref, w1_ref, w2_ref, head_ref, up_bias_ref, first_bias_ref,
    second_bias_ref, head_bias_ref, mask_ref, target_ref, terms_ref, ends_ref, piece_ref, second_ref,
    one_ref, two_ref, recv_ref, far_ref, across_ref, flux_ref, send_ref, sems,
):
    tile = lax.axis_index("tile")
    bottom = tile == lax.axis_size("tile") - 1
    top = tile == 0
    even_tile = lax.rem(tile, 2) == 0
    even_face = lax.rem(lax.axis_index("face"), 2) == 0

    def loads(member):
        return [
            pltpu.make_async_copy(first_hbm.at[member], first_ref.at[member], sems.at[0, member]),
            pltpu.make_async_copy(part_hbm.at[member], part_ref.at[member], sems.at[1, member]),
        ]

    small = [
        pltpu.make_async_copy(source, target, sems.at[2, k])
        for k, (source, target) in enumerate(
            [
                (one_hbm, one_ref),
                (two_hbm, two_ref),
                (across_hbm, across_ref),
                (far_hbm, far_ref),
                (recv_hbm.at[31], recv_ref.at[31]),
                (up_w_hbm, up_w_ref),
                (w1_hbm, w1_ref),
                (w2_hbm, w2_ref),
                (head_hbm, head_ref),
                (up_bias_hbm, up_bias_ref),
                (first_bias_hbm, first_bias_ref),
                (second_bias_hbm, second_bias_ref),
                (head_bias_hbm, head_bias_ref),
                (mask_hbm, mask_ref),
                (target_hbm, target_ref),
                (cols_hbm, cols_ref),
            ]
        )
    ]
    chunks = pltpu.make_async_copy(
        recv_hbm.at[pl.ds(0, 31)], recv_ref.at[pl.ds(0, 31)], sems.at[3, 0]
    )

    def store_flux(member):
        return [pltpu.make_async_copy(flux_ref.at[member], flux_hbm.at[member], sems.at[3, 1 + member])]

    @pl.when(bottom)
    def _():
        chunks.start()

    begin(small)
    begin(loads(0))
    begin(loads(1))
    finish(small)
    begin(loads(2))

    @pl.when(bottom)
    def _():
        chunks.wait()

    up_bias = bias_column(up_bias_ref, 64)
    up_bias_wide = wide(up_bias, 4)
    first_bias = bias_column(first_bias_ref, 64)
    first_bias_wide = wide(first_bias, 4)
    second_bias_wide = wide(bias_column(second_bias_ref, 64), 4)
    head_bias = wide(bias_column(head_bias_ref, 8), 4)
    lane = lanes_of((128, 128))
    place = lax.rem(lane, 32)
    lane64 = lanes_of((64, 128))
    place64 = lax.rem(lane64, 32)
    zero = jnp.zeros((128, 128), F32)
    ghost_rows = jnp.zeros((32, 128), F32)

    by_row = [row_taps(w1_ref, r) for r in range(3)]
    above = jnp.where(even_tile, two_ref[...], one_ref[...])
    above = jnp.where(top, jnp.zeros_like(above), above)

    @pl.when(jnp.logical_not(bottom))
    def _():
        below = jnp.where(even_tile, one_ref[...], two_ref[...]).astype(F32)
        for member in range(3):
            for k in range(4):
                terms_ref[member, 2, :, 128 * k : 128 * k + 128] = below[8 * member + k]
                terms_ref[member, 3, :, 128 * k : 128 * k + 128] = below[8 * member + 4 + k]
            ends_ref[member] = pltpu.roll(below[24], (128 - 4 * member) % 128, 1)
        piece_ref[...] = recv_ref[31].astype(F32)

    @pl.when(bottom)
    def _():
        near, far = two_ref[16:19].reshape(192, 128), far_ref[...]
        from_previous = jnp.where(even_face, far[:96], near[:96])
        turned_up = jnp.concatenate(
            [jnp.concatenate([up_w_ref[0, 1 - q], up_w_ref[1, 1 - q]], axis=1) for q in range(2)], axis=0
        )
        near_weight = jnp.concatenate([by_row[2], turned_taps(w1_ref, 1)], axis=0)
        far_weight = turned_taps(w1_ref, 2)
        for member in range(3):
            own = slice(32 * member, 32 * member + 32)
            pieces = [recv_ref[j].astype(F32)[own] for j in range(31)]
            pieces.append(from_previous.astype(F32)[own])
            skip = jnp.concatenate(
                [
                    jnp.concatenate([pieces[8 * q + j][:16] for j in range(8)], axis=0).T.astype(BF)
                    for q in range(4)
                ],
                axis=1,
            )
            coarse = jnp.concatenate(
                [
                    jnp.concatenate([pieces[16 * q + j][16:24] for j in range(16)], axis=0).T
                    for q in range(2)
                ],
                axis=1,
            )
            fine = dot(turned_up, spread(coarse))
            beyond = [
                jnp.concatenate(
                    [(fine[64 * a : 64 * a + 64] + up_bias_wide).astype(BF), skip[64 * a : 64 * a + 64]], axis=0
                )
                for a in range(2)
            ]
            terms = dot(near_weight, taps(beyond[0]))
            terms_ref[member, 2] = terms[:64]
            terms_ref[member, 3] = terms[64:] + dot(far_weight, taps(beyond[1]))
            ends_ref[member] = jnp.zeros((64, 128), F32)
        piece_ref[...] = jnp.where(even_face, near[96:], far[96:]).astype(F32)

    edge = cols_ref[:128]
    for member in range(3):
        end = pltpu.roll(above[24].astype(F32), (128 - 4 * member) % 128, 1)
        for k in range(4):
            terms_ref[member, 0, :, 128 * k : 128 * k + 128] = above[8 * member + 4 + k].astype(F32)
            terms_ref[member, 1, :, 128 * k : 128 * k + 128] = above[8 * member + k].astype(F32)
        for x, ends in ((0, end), (18, ends_ref[member])):
            for a in range(2):
                target = 32 * member + x + a
                moved = jnp.concatenate(
                    [pltpu.roll(ends, (target - 2 * a - h) % 128, 1) for h in range(2)], axis=0
                )
                edge = jnp.where(lane == target, moved, edge)

    pixel = tile * ROWS - 2 + place
    piece = jnp.concatenate([piece_ref[...], ghost_rows], axis=0).T
    doubled = jnp.take_along_axis(piece, jnp.minimum(lane - place + 20 + lax.div(place, 2), 127), axis=1)
    even = lax.rem(lane, 2) == 0
    spread_piece = jnp.concatenate(
        [jnp.where(even, doubled, zero), jnp.where(even, zero, doubled)], axis=0
    ).astype(BF)
    ghost_up = jnp.concatenate(
        [jnp.concatenate([up_w_ref[1 - q, 0], up_w_ref[1 - q, 1]], axis=1) for q in range(2)], axis=0
    )
    ghost_fine = dot(ghost_up, spread_piece)
    inside = (place < 20) & (pixel >= 0) & (pixel < COLS) & (lane < 96)
    ghost = []
    for q in range(2):
        upsampled = (ghost_fine[64 * q : 64 * q + 64] + up_bias).astype(BF).astype(F32)
        joined = jnp.concatenate([upsampled, piece[64 * q : 64 * q + 64]], axis=0)
        ghost.append(jnp.where(inside, joined, zero))

    corner = jnp.concatenate([across_ref[...].astype(F32), ghost_rows], axis=0).T
    at_corner = dot(
        jnp.concatenate([up_w_ref[1, 1], up_w_ref[1, 0], up_w_ref[0, 1]], axis=0), corner.astype(BF)
    )
    held = (place == 18) & bottom & (lane < 96)

    def corner_column(k, q, x):
        upsampled = (at_corner[64 * k : 64 * k + 64] + up_bias).astype(BF).astype(F32)
        joined = jnp.concatenate(
            [pltpu.roll(upsampled, 123, 1), pltpu.roll(corner[64 * q : 64 * q + 64], 18 - x, 1)], axis=0
        )
        return jnp.where(held, joined, zero)

    corner0 = corner_column(0, 0, 15)
    corner1 = corner_column(1, 1, 15)
    corner2 = corner_column(2, 0, 14)

    def around(joined):
        return [pltpu.roll(joined, 1, 1), joined, pltpu.roll(joined, 127, 1)]

    weight = jnp.concatenate([w1_ref[r, 2] for r in range(3)], axis=1)
    added = dot(weight, jnp.concatenate(around(ghost[0].astype(BF)), axis=0))
    weight = jnp.concatenate([w1_ref[2, 1], w1_ref[2, 0]], axis=1)
    added_bottom = dot(weight, jnp.concatenate([corner0, corner2], axis=0).astype(BF))
    added = jnp.where((place64 == 18) & bottom, added_bottom, added)

    edge = jnp.where((place == 18) & bottom, zero, edge)
    columns = [edge.astype(BF), (ghost[0] + corner0).astype(BF), (ghost[1] + corner1).astype(BF)]
    weight = jnp.concatenate([w1_ref[2 - s, r] for s in range(3) for r in range(3)], axis=1)
    summed = dot(weight, jnp.concatenate([part for joined in columns for part in around(joined)], axis=0))
    pixel64 = tile * ROWS - 2 + place64
    inside64 = (place64 >= 1) & (place64 <= 18) & (pixel64 >= 0) & (pixel64 < COLS)
    first_ghost = jnp.where(inside64, silu(summed + first_bias), jnp.zeros((64, 128), F32))
    last = silu(cols_ref[128:] + added)

    second_weight = jnp.concatenate([row_taps(w2_ref, r) for r in range(3)], axis=0)
    head = head_ref[...]
    lane512 = lanes_of((64, COLS))

    def one(member, carry):
        base = 125 - 32 * member

        def finished(summed, x):
            end = summed[:, 384:512] + jnp.where(lane64 == 127, pltpu.roll(added, base - x, 1), 0.0)
            summed = jnp.concatenate([summed[:, :384], end], axis=1)
            return silu(summed + first_bias_wide).astype(BF)

        finish(loads(member))
        row_m1, row_0, row_15, row_16 = (
            finished(part_ref[member, k] + terms_ref[member, k], x) for k, x in enumerate((-1, 0, 15, 16))
        )
        outer = {-1: jnp.where(top, jnp.zeros_like(row_m1), row_m1), 0: row_0, 15: row_15, 16: row_16}

        before = [None, None]
        for x in range(-1, ROWS + 1):
            if x in outer:
                row = outer[x]
            else:
                row = first_ref[member, x]
                end = jnp.where(lane64 == 127, pltpu.roll(last, base - x, 1).astype(BF), row[:, 384:512])
                row = jnp.concatenate([row[:, :384], end], axis=1)
            moved = pltpu.roll(row, COLS - 1, 1)
            end = jnp.where(
                lane64 == 127, pltpu.roll(first_ghost, base - x, 1).astype(BF), moved[:, 384:512]
            )
            after = jnp.concatenate([moved[:, :384], end], axis=1)
            first_part = jnp.where(lane512 == 0, jnp.zeros_like(row), pltpu.roll(row, 1, 1))
            summed = dot(second_weight, jnp.concatenate([first_part, row, after], axis=0))
            low, mid, high = summed[:64], summed[64:128], summed[128:]
            done = high if before[0] is None else before[0] + high
            before = [mid if before[1] is None else before[1] + mid, low]
            n = x - 1
            if n >= 0:
                second_ref[n] = silu(done + second_bias_wide).astype(BF)
        for n in range(ROWS):
            flux_ref[member, :, n, :] = dot(head, second_ref[n]) + head_bias
        begin(store_flux(member))
        return carry

    lax.fori_loop(0, 3, one, 0)

    target = target_ref[...]
    owner = jnp.where(target >= 0, lax.div(jnp.maximum(target, 0), CAP), -1)
    slot = jnp.where(target >= 0, target - owner * CAP + 1, 0)
    wanted = lax.broadcasted_iota(jnp.int32, (128, 64), 0)
    by_pixel_row = jnp.where(jnp.broadcast_to(owner, (128, 64)) == wanted, 1.0, 0.0).astype(BF)
    block = lax.broadcasted_iota(jnp.int32, (64, 64), 0)
    place = lax.broadcasted_iota(jnp.int32, (64, 64), 1)
    moved = jnp.where(block == 4 * lax.rem(place, 16) + lax.div(place, 16), 1.0, 0.0).astype(BF)
    chosen = dot(by_pixel_row, moved).astype(BF)
    mask = mask_ref[...].astype(F32)
    packed = []
    for member in range(3):
        for k in range(8):
            masked = (flux_ref[member, k] * mask).astype(BF)
            blocks = jnp.concatenate([masked[:, 128 * q : 128 * q + 128] for q in range(4)], axis=0)
            packed.append(dot(chosen, blocks).astype(BF))
    slots = jnp.broadcast_to(slot.astype(F32), (128, 64)).astype(BF)
    slots = jnp.sum(by_pixel_row.astype(F32) * slots.astype(F32), axis=1, keepdims=True)
    slots = jnp.broadcast_to(slots, (128, 128)).astype(BF)
    packed += [slots] * 8
    packed = jnp.stack(packed, axis=0)
    sends = []
    for k in range(2):
        part = slice(64 * k, 64 * k + 64)
        send_ref[part] = jnp.swapaxes(packed[:, part], 0, 1)
        half = pl.ds(64 * k, 64)
        sends.append(pltpu.make_async_copy(send_ref.at[half], send_hbm.at[half], sems.at[3, 4 + k]))
        sends[k].start()
    for member in range(3):
        finish(store_flux(member))
    finish(sends)


def unpack_kernel(recv_ref, out_ref):
    rows = jnp.swapaxes(recv_ref[...], 0, 1)
    slots = rows[24].astype(F32).T[:48]
    wanted = (lax.broadcasted_iota(jnp.int32, slots.shape, 0) + 1).astype(F32)
    chosen = jnp.where(slots == wanted, 1.0, 0.0).astype(BF)
    for k in range(24):
        out_ref[:, k, :] = dot(chosen, rows[k])[:CAP]


def vmem(count):
    return [pl.BlockSpec(memory_space=pltpu.VMEM)] * count


def hbm(count):
    return [pl.BlockSpec(memory_space=pltpu.HBM)] * count


def shards(
    coarse_features,
    skip_features,
    up_weight,
    up_bias,
    first_weight,
    first_bias,
    second_weight,
    second_bias,
    head_weight,
    head_bias,
    land_mask,
    block_target,
):
    faces = lax.axis_size("face")
    tiles = lax.axis_size("tile")
    devices = faces * tiles
    params = pltpu.CompilerParams(vmem_limit_bytes=VMEM_LIMIT)
    sds = jax.ShapeDtypeStruct

    up_bias, first_bias, second_bias = (b.reshape(1, 64) for b in (up_bias, first_bias, second_bias))
    one, two, send, col, edges = pl.pallas_call(
        pack_kernel,
        in_specs=hbm(5),
        out_specs=hbm(3) + vmem(2),
        out_shape=[
            sds((25, 64, 128), BF),
            sds((25, 64, 128), BF),
            sds((32, 96, 128), BF),
            sds((96, 128), BF),
            sds((192, 128), BF),
        ],
        scratch_shapes=[
            pltpu.VMEM((3, 128, 8, 256), BF),
            pltpu.VMEM((3, 64, 16, 512), BF),
            pltpu.VMEM((2, 2, 64, 128), BF),
            pltpu.VMEM((3, 3, 64, 128), BF),
            pltpu.VMEM((1, 64), F32),
            pltpu.VMEM((25, 64, 128), BF),
            pltpu.VMEM((25, 64, 128), BF),
            pltpu.VMEM((32, 96, 128), BF),
            pltpu.VMEM((544, 128), F32),
            pltpu.VMEM((272, 128), F32),
            pltpu.SemaphoreType.DMA((6, 3)),
        ],
        compiler_params=params,
        name="pack_edges",
    )(coarse_features, skip_features, up_weight, first_weight, up_bias)

    last = tiles - 1

    both = ("face", "tile")

    def swapped(bits):
        return [(f * tiles + last, (f ^ bits) * tiles + last) for f in range(faces)]

    strips = [f * tiles for f in range(faces)]
    first_pairs = [(s + t, s + (t ^ 1)) for s in strips for t in range(tiles)]
    second_pairs = [(s + t, s + ((t - 1) ^ 1) + 1) for s in strips for t in range(1, last)]
    got_one = lax.ppermute(one, both, first_pairs)
    got_two = lax.ppermute(two, both, second_pairs + swapped(1) + [(f * tiles, (f ^ 1) * tiles) for f in range(faces)])
    far = lax.ppermute(edges, "face", [(f, f ^ 3) for f in range(faces)])
    across = lax.ppermute(col, "face", [(f, f ^ 2) for f in range(faces)])
    groups = [
        [f * tiles + t for t in range(last)] + [((f + 1) % faces) * tiles + last] for f in range(faces)
    ]
    recv = lax.all_to_all(send, both, 0, 0, axis_index_groups=groups, tiled=True)

    first, parts, cols = pl.pallas_call(
        inner_kernel,
        in_specs=hbm(6),
        out_specs=hbm(3),
        out_shape=[sds((3, 16, 64, 512), BF), sds((3, 4, 64, 512), F32), sds((192, 128), F32)],
        scratch_shapes=[
            pltpu.VMEM((3, 128, 8, 256), BF),
            pltpu.VMEM((3, 64, 16, 512), BF),
            pltpu.VMEM((2, 2, 64, 128), BF),
            pltpu.VMEM((3, 3, 64, 128), BF),
            pltpu.VMEM((1, 64), F32),
            pltpu.VMEM((1, 64), F32),
            pltpu.VMEM((3, 16, 64, 512), BF),
            pltpu.VMEM((3, 4, 64, 512), F32),
            pltpu.VMEM((192, 128), F32),
            pltpu.VMEM((16, 128, 512), BF),
            pltpu.SemaphoreType.DMA((6, 4)),
        ],
        compiler_params=params,
        name="inner_rows",
    )(coarse_features, skip_features, up_weight, first_weight, up_bias, first_bias)

    flux, send = pl.pallas_call(
        edge_kernel,
        in_specs=hbm(18),
        out_specs=hbm(2),
        out_shape=[sds((3, 8, 16, 512), F32), sds((devices, 32, 128), BF)],
        scratch_shapes=[
            pltpu.VMEM((3, 16, 64, 512), BF),
            pltpu.VMEM((3, 4, 64, 512), F32),
            pltpu.VMEM((192, 128), F32),
            pltpu.VMEM((2, 2, 64, 128), BF),
            pltpu.VMEM((3, 3, 64, 128), BF),
            pltpu.VMEM((3, 3, 64, 64), BF),
            pltpu.VMEM((8, 64), BF),
            pltpu.VMEM((1, 64), F32),
            pltpu.VMEM((1, 64), F32),
            pltpu.VMEM((1, 64), F32),
            pltpu.VMEM((1, 8), F32),
            pltpu.VMEM((16, 512), jnp.int32),
            pltpu.VMEM((1, 64), jnp.int32),
            pltpu.VMEM((3, 4, 64, 512), F32),
            pltpu.VMEM((3, 64, 128), F32),
            pltpu.VMEM((96, 128), F32),
            pltpu.VMEM((16, 64, 512), BF),
            pltpu.VMEM((25, 64, 128), BF),
            pltpu.VMEM((25, 64, 128), BF),
            pltpu.VMEM((32, 96, 128), BF),
            pltpu.VMEM((192, 128), BF),
            pltpu.VMEM((96, 128), BF),
            pltpu.VMEM((3, 8, 16, 512), F32),
            pltpu.VMEM((128, 32, 128), BF),
            pltpu.SemaphoreType.DMA((4, 16)),
        ],
        compiler_params=params,
        name="edges_and_second",
    )(
        first, parts, cols, got_one, got_two, recv, far, across,
        up_weight, first_weight, second_weight, head_weight, up_bias, first_bias, second_bias,
        head_bias.reshape(1, 8), land_mask, block_target.reshape(1, 64),
    )

    got = lax.all_to_all(send, both, 0, 0, tiled=True)
    ocean = pl.pallas_call(
        unpack_kernel,
        in_specs=vmem(1),
        out_specs=vmem(1)[0],
        out_shape=sds((CAP, 24, 128), F32),
        compiler_params=pltpu.CompilerParams(vmem_limit_bytes=UNPACK_LIMIT),
        name="ocean_slots",
    )(got)
    return flux, ocean.reshape(CAP, 3, 8, 128)


def solution(mesh):
    placed = (
        P(None, None, ("face", "tile"), None),
        P(None, None, ("face", "tile"), None),
        P(),
        P(),
        P(),
        P(),
        P(),
        P(),
        P(),
        P(),
        P(("face", "tile"), None),
        P(("face", "tile")),
    )
    return jax.shard_map(
        shards,
        mesh=mesh,
        in_specs=placed,
        out_specs=(P(None, None, ("face", "tile"), None), P(("face", "tile"), None, None, None)),
        check_vma=False,
    )
```
